256 devices in a mesh: dp: 32 (over x, y, core), expert: 8 (over z).
Axes of the slice: x: 4, y: 4, z: 8, core: 2. Of those that a mesh axis runs over, the one named last changes fastest.
Arguments:
- tokens: float32 [32768, 1280], P(('dp', 'expert')), may hold values from -6 to 6
- router_weight: float32 [1280, 32], replicated, may hold values from -0.3125 to 0.3125
- expert_in: float32 [32, 1280, 2560], P('dp', None, 'expert'), may hold values from -0.15625 to 0.15625
- expert_out: float32 [32, 2560, 1280], P('dp', 'expert'), may hold values from -0.125 to 0.125
- projection: float32 [2, 1280, 512], P(None, 'expert'), may hold values from -0.15625 to 0.15625
- assignment: int32 [32768], P(('dp', 'expert')), may hold values from 0 to 31, as said below
- modality: int32 [32768], P(('dp', 'expert')), may hold values from 0 to 1, as said below
Outputs:
- losses: float32 [3], replicated
- grad_tokens: float32 [32768, 1280], P(('dp', 'expert'))
- grad_router: float32 [1280, 32], replicated
- grad_expert_in: float32 [32, 1280, 2560], P('dp', None, 'expert')
- grad_expert_out: float32 [32, 2560, 1280], P('dp', 'expert')
- grad_projection: float32 [2, 1280, 512], P(None, 'expert')
The draws below stay inside these ranges and needn't reach their ends.
Inputs may be any that keep to these rules, and one draw needn't show every extreme that they name: `assignment`: within each aligned block of 128 tokens (the tokens of one device) no expert is named by more than 5 tokens. In every block some expert is named exactly 5 times, and one expert is named 5 times in every block. Each aligned block of 128 tokens is one image-text pair: its image tokens come first, and it holds at least 16 tokens of each modality.
All inputs are finite; a program needn't handle non-finite values.
Results may differ from the reference program's by a relative error of at most 0.00013.
Values sent between devices are 32-bit elements; how exact they have to be, the bound alone decides.
No kernel may reach another device: no remote copies, remote signals or barrier semaphores. Data moves between devices by JAX's collectives and lax.ppermute only.
A program may use at most 192 MiB of HBM per device.

```python
import jax
import jax.numpy as jnp
from jax import lax

D = 1280
FF = 2560
EMB = 512
PAIR_LEN = 128
EXPERTS = 32
TOK_DEV = 128
TOKENS = 32768
PAIRS = 256
CAP = 5


def routing_table(key):
    blocks = TOKENS // TOK_DEV
    cells = EXPERTS * CAP
    common = jax.random.randint(jax.random.fold_in(key, 11), (), 0, EXPERTS)

    def one_block(index):
        block_key = jax.random.fold_in(key, index + 1000)
        pick_key, order_key, shuffle_key = jax.random.split(block_key, 3)
        second = jax.random.randint(pick_key, (), 0, EXPERTS)
        order = jax.random.permutation(order_key, cells).astype(jnp.int32)
        owner = jnp.arange(cells, dtype=jnp.int32) % EXPERTS
        forced = (owner == common) | (owner == second)
        ranking = jnp.where(forced, order - cells, order)
        chosen = jnp.argsort(ranking)[:TOK_DEV]
        return jax.random.permutation(shuffle_key, chosen)
    return jax.vmap(one_block)(jnp.arange(blocks, dtype=jnp.int32)).reshape(-1).astype(jnp.int32)


def draw_assignment(key, part):
    table = routing_table(key)
    return (table % EXPERTS).astype(jnp.int32)


def draw_modality(key, part):
    key = jax.random.fold_in(key, 7)
    pair_index = jnp.arange(PAIRS, dtype=jnp.int32)
    span = max(PAIRS - 1, 1)
    extra = jax.random.randint(key, (PAIRS,), 0, PAIR_LEN // 8 + 1)
    images = PAIR_LEN // 8 + pair_index * (5 * PAIR_LEN // 8) // span + extra
    position = jnp.arange(PAIR_LEN, dtype=jnp.int32)
    return (position[None, :] >= images[:, None]).astype(jnp.int32).reshape(-1)


def steps_of(stream_key, dims, pieces, least, largest):
    def one(dim, shards_of):
        steps = jax.random.uniform(jax.random.fold_in(jax.random.fold_in(stream_key, 6), dim), (shards_of,), jnp.float32, least / len(pieces), largest / len(pieces))
        return jnp.repeat(jnp.exp(steps), dims[dim] // shards_of).reshape((-1,) + (1,) * (len(dims) - dim - 1))

    level = one(*pieces[0])
    for cut in pieces[1:]:
        level = level * one(*cut)
    return level


def noise(stream_key, dims, deviation, limit, shards=(), held_as=jnp.bfloat16):
    gain = steps_of(stream_key, dims, shards, -0.22, 0.18) if shards else 1.0
    array = jax.random.normal(stream_key, dims, jnp.float32) * deviation * gain
    return jnp.minimum(jnp.maximum(array, -limit), limit).astype(held_as)


def setup_inputs(seed: int = 0) -> dict:
    arg_keys = jax.random.split(jax.random.key(seed), 8)
    return {
        "tokens": noise(arg_keys[0], (TOKENS, D), 1.0, 6.0, ((0, 256),), jnp.float32),
        "router_weight": noise(arg_keys[1], (D, EXPERTS), (D // 4) ** -0.5, 0.3125, (), jnp.float32),
        "expert_in": noise(arg_keys[2], (EXPERTS, D, FF), D ** -0.5, 0.15625, ((0, 32), (2, 8)), jnp.float32),
        "expert_out": noise(arg_keys[3], (EXPERTS, FF, D), FF ** -0.5, 0.125, ((0, 32), (1, 8)), jnp.float32),
        "projection": noise(arg_keys[4], (2, D, EMB), D ** -0.5, 0.15625, ((1, 8),), jnp.float32),
        "assignment": draw_assignment(jax.random.fold_in(arg_keys[7], 71), 0),
        "modality": draw_modality(jax.random.fold_in(arg_keys[7], 71), 0),
    }


def forward(tokens, router_weight, expert_in, expert_out, projection, assignment, modality):
    highest = lax.Precision.HIGHEST
    blocks = TOKENS // TOK_DEV
    logits = jnp.dot(tokens, router_weight, precision=highest)
    exponent = jnp.exp(logits)
    router_prob = exponent / lax.optimization_barrier(jnp.sum(exponent, axis=1, keepdims=True))
    expert_ids = jnp.arange(EXPERTS, dtype=jnp.int32)
    chosen_int = (assignment[:, None] == expert_ids[None, :]).astype(jnp.int32)
    chosen_mask = chosen_int.astype(jnp.float32)
    gate_value = lax.optimization_barrier(jnp.sum(router_prob * chosen_mask, axis=1))
    block_choice = chosen_int.reshape(blocks, TOK_DEV, EXPERTS)
    earlier = jnp.cumsum(block_choice, axis=1).astype(jnp.int32) - block_choice
    slot = lax.optimization_barrier(jnp.sum(earlier * block_choice, axis=2)).reshape(TOKENS).astype(jnp.int32)
    cell_ids = jnp.arange(CAP * EXPERTS, dtype=jnp.int32)
    onehot = ((slot * EXPERTS + assignment)[:, None] == cell_ids[None, :]).astype(jnp.float32)
    onehot = onehot.reshape(blocks, TOK_DEV, CAP * EXPERTS)
    block_rows = tokens.reshape(blocks, TOK_DEV, D)
    dispatched = jnp.einsum('btc,btd->bcd', onehot, block_rows, precision=highest)
    routed = jnp.transpose(dispatched.reshape(blocks, CAP, EXPERTS, D), (2, 0, 1, 3)).reshape(EXPERTS, blocks * CAP, D)
    hidden = jax.nn.gelu(jnp.einsum('erd,edf->erf', routed, expert_in, precision=highest), approximate=False)
    result = jnp.einsum('erf,efd->erd', hidden, expert_out, precision=highest)
    returned = jnp.transpose(result.reshape(EXPERTS, blocks, CAP, D), (1, 2, 0, 3)).reshape(blocks, CAP * EXPERTS, D)
    combined = jnp.einsum('btc,bcd->btd', onehot, returned, precision=highest).reshape(TOKENS, D)
    output = tokens + gate_value[:, None] * combined
    is_image = (modality == 0).astype(jnp.float32)
    modal_mask = jnp.stack([is_image, 1.0 - is_image], axis=1)
    pair_mask = modal_mask.reshape(PAIRS, PAIR_LEN, 2)
    group_sizes = lax.optimization_barrier(jnp.sum(pair_mask, axis=1))
    pooled = jnp.einsum('plm,pld->pmd', pair_mask, output.reshape(PAIRS, PAIR_LEN, D), precision=highest) / group_sizes[:, :, None]
    embedding = jnp.einsum('pmd,mde->pme', pooled, projection, precision=highest)
    unit_embed = embedding / jnp.sqrt(lax.optimization_barrier(jnp.sum(embedding * embedding, axis=2, keepdims=True)) + 1e-06)
    scores = 10.0 * jnp.einsum('ie,je->ij', unit_embed[:, 0], unit_embed[:, 1], precision=highest)
    row_terms = jnp.log(lax.optimization_barrier(jnp.sum(jnp.exp(scores), axis=1)))
    column_terms = jnp.log(lax.optimization_barrier(jnp.sum(jnp.exp(scores), axis=0)))
    contrast = (jnp.sum(row_terms) + jnp.sum(column_terms) - 2.0 * jnp.sum(jnp.diagonal(scores))) / (2.0 * PAIRS)
    counts = lax.optimization_barrier(jnp.sum(modal_mask, axis=0))
    mean_usage = jnp.einsum('tm,te->me', modal_mask, router_prob, precision=highest) / counts[:, None]
    entropy = lax.optimization_barrier(jnp.sum(mean_usage * jnp.log(mean_usage), axis=1))
    objective = TOKENS * (contrast + 0.5 * (entropy[0] + entropy[1]))
    return (objective, (contrast, entropy[0], entropy[1]))

def reference(tokens, router_weight, expert_in, expert_out, projection, assignment, modality):

    def objective_of(tokens, router_weight, expert_in, expert_out, projection):
        return forward(tokens, router_weight, expert_in, expert_out, projection, assignment, modality)
    objective, backward, extras = jax.vjp(objective_of, tokens, router_weight, expert_in, expert_out, projection, has_aux=True)
    grads = backward(jnp.ones_like(objective))
    losses = jnp.stack([extras[0], extras[1], extras[2]])
    return (losses, grads[0], grads[1], grads[2], grads[3], grads[4])
```

```python
import jax
import jax.numpy as jnp
from jax import lax
from jax.sharding import PartitionSpec as P

highest = lax.Precision.HIGHEST
high = lax.Precision.HIGH
contrast_scale = 10.0
entropy_weight = 0.5
norm_epsilon = 1e-06
CAP = 5


def gelu_exact(values):
    return jax.nn.gelu(values, approximate=False)


def dot(a, b, dims, precision=high):
    return lax.dot_general(a, b, (dims, ((), ())), precision=precision)


def mm(a, b, precision=high):
    return dot(a, b, ((1,), (0,)), precision)


def mm_nt(a, b, precision=high):
    return dot(a, b, ((1,), (1,)), precision)


def mm_tn(a, b, precision=high):
    return dot(a, b, ((0,), (0,)), precision)


def a2a(values, axis_name, axis):
    return lax.all_to_all(values, axis_name, split_axis=axis, concat_axis=axis, tiled=True)


def gather(values, axis_name):
    return lax.all_gather(values, axis_name, axis=0, tiled=True)


def body(tokens, router_weight, expert_in, expert_out, projection, assignment, modality):
    tok_count, width = tokens.shape
    experts = router_weight.shape[1]
    n_dp = lax.axis_size("dp")
    n_z = lax.axis_size("expert")
    pairs = n_dp * n_z
    total_tokens = tok_count * pairs
    w_in = expert_in[0]
    w_out = expert_out[0]
    hidden_dev = w_in.shape[1]
    embed_width = projection.shape[2]
    my_dp = lax.axis_index("dp")
    my_z = lax.axis_index("expert")
    own_pair = my_z * n_dp + my_dp
    my_core = my_dp % 2

    projection_mine = gather(jnp.where(my_core == 0, projection[0], projection[1]), "expert")
    projection_other = lax.ppermute(projection_mine, "dp", [(i, i ^ 1) for i in range(n_dp)])

    expert_ids = lax.broadcasted_iota(jnp.int32, (1, experts), 1)
    chosen_mask = (assignment[:, None] == expert_ids).astype(jnp.float32)
    before = (
        lax.broadcasted_iota(jnp.int32, (tok_count, tok_count), 0)
        > lax.broadcasted_iota(jnp.int32, (tok_count, tok_count), 1)
    ).astype(jnp.bfloat16)
    earlier = jnp.dot(
        before, chosen_mask.astype(jnp.bfloat16), preferred_element_type=jnp.float32
    )
    slot = jnp.sum(earlier * chosen_mask, axis=1).astype(jnp.int32)
    cell_ids = lax.broadcasted_iota(jnp.int32, (1, CAP * experts), 1)
    onehot = ((slot * experts + assignment)[:, None] == cell_ids).astype(jnp.float32)
    dispatched = mm_tn(onehot, tokens, highest).reshape(CAP, experts, width)
    received = a2a(dispatched, "dp", 1).reshape(CAP * n_dp, width)
    rows = gather(received, "expert")

    logits = mm(tokens, router_weight, highest)
    exponent = jnp.exp(logits)
    router_prob = exponent / jnp.sum(exponent, axis=1, keepdims=True)
    is_image = (modality == 0).astype(jnp.float32)
    modal_mask = jnp.stack([is_image, 1.0 - is_image], axis=0)
    images = jnp.sum(is_image)
    group_sizes = jnp.stack([images, tok_count - images])
    usage_part = mm(modal_mask, router_prob, highest).reshape(1, 2 * experts)
    image_slots = dot(chosen_mask, is_image, ((0,), (0,)), highest)
    meta = jnp.concatenate(
        [
            image_slots[:, None],
            jnp.broadcast_to(images, (experts, 1)),
            jnp.broadcast_to(usage_part, (experts, 2 * experts)),
            jnp.zeros((experts, 126 - 2 * experts), jnp.float32),
        ],
        axis=1,
    )
    meta, received_late = lax.optimization_barrier((meta, received[:1, :1]))
    meta_all = gather(a2a(meta, "dp", 0), "expert")
    token_means = mm(modal_mask / group_sizes[:, None], tokens, highest)

    projection_img = jnp.where(my_core == 0, projection_mine, projection_other)
    projection_txt = jnp.where(my_core == 0, projection_other, projection_mine)
    mixed_img = mm(w_out, projection_img)
    mixed_txt = mm(w_out, projection_txt)
    embed_means = jnp.concatenate(
        [mm(token_means[:1], projection_img), mm(token_means[1:], projection_txt)], axis=0
    )

    usage_all = jnp.sum(meta_all[:, 2 : 2 + 2 * experts], axis=0).reshape(2, experts)
    images_of = meta_all[:, 1]
    image_total = jnp.sum(images_of)
    count_sum = jnp.stack([image_total, total_tokens - image_total])
    slot_ids = lax.broadcasted_iota(jnp.int32, (1, CAP, 1), 1).astype(jnp.float32)
    in_image = slot_ids < meta_all[:, 0].reshape(n_z, 1, n_dp)
    weight_img = jnp.where(in_image, 1.0 / images_of.reshape(n_z, 1, n_dp), 0.0)
    weight_txt = jnp.where(in_image, 0.0, 1.0 / (tok_count - images_of).reshape(n_z, 1, n_dp))

    pre = mm(rows, w_in)
    row_exponent = jnp.exp(mm(rows, router_weight))
    row_prob = row_exponent / jnp.sum(row_exponent, axis=1, keepdims=True)
    my_expert = (expert_ids == my_dp).astype(jnp.float32)
    row_gate = jnp.sum(row_prob * my_expert, axis=1).reshape(n_z, CAP, n_dp)
    hidden, gelu_back = jax.vjp(gelu_exact, pre)
    hidden_rows = hidden.reshape(n_z, CAP, n_dp, hidden_dev)
    gate_img = (row_gate * weight_img)[..., None]
    gate_txt = (row_gate * weight_txt)[..., None]
    sum_img = jnp.sum(hidden_rows * gate_img, axis=1).reshape(pairs, hidden_dev)
    sum_txt = jnp.sum(hidden_rows * gate_txt, axis=1).reshape(pairs, hidden_dev)

    part = jnp.stack(
        [
            mm(sum_img, mixed_img).reshape(n_z, n_dp, embed_width),
            mm(sum_txt, mixed_txt).reshape(n_z, n_dp, embed_width),
        ],
        axis=1,
    )
    part = jnp.sum(a2a(part, "expert", 0), axis=0)
    embedding = jnp.sum(a2a(part, "dp", 1), axis=1) + embed_means
    column = lax.all_gather(embedding, "dp", axis=1, tiled=False)
    every = gather(column[None], "expert")
    embed_img = every[:, 0].reshape(pairs, embed_width)
    embed_txt = every[:, 1].reshape(pairs, embed_width)

    def normalized(values):
        radius = jnp.sqrt(jnp.sum(values * values, axis=1, keepdims=True) + norm_epsilon)
        return values / radius, radius

    unit_img, radius_img = normalized(embed_img)
    unit_txt, radius_txt = normalized(embed_txt)
    scores = contrast_scale * mm_nt(unit_img, unit_txt, highest)
    exp_scores = jnp.exp(scores)
    total_img = jnp.sum(exp_scores, axis=1, keepdims=True)
    total_txt = jnp.sum(exp_scores, axis=0, keepdims=True)
    diagonal = (
        lax.broadcasted_iota(jnp.int32, (pairs, pairs), 0)
        == lax.broadcasted_iota(jnp.int32, (pairs, pairs), 1)
    ).astype(jnp.float32)
    contrast = (
        jnp.sum(jnp.log(total_img)) + jnp.sum(jnp.log(total_txt)) - 2.0 * jnp.sum(scores * diagonal)
    ) / (2.0 * pairs)
    coupling = (exp_scores / total_img + exp_scores / total_txt - 2.0 * diagonal) * (
        contrast_scale * total_tokens / (2.0 * pairs)
    )

    def embed_back(unit, radius, grad_unit):
        return (grad_unit - unit * jnp.sum(unit * grad_unit, axis=1, keepdims=True)) / radius

    grad_img = embed_back(unit_img, radius_img, mm(coupling, unit_txt, highest))
    grad_txt = embed_back(unit_txt, radius_txt, mm_tn(coupling, unit_img, highest))

    back_img = mm_nt(grad_img, mixed_img).reshape(n_z, 1, n_dp, hidden_dev)
    back_txt = mm_nt(grad_txt, mixed_txt).reshape(n_z, 1, n_dp, hidden_dev)
    grad_hidden = gate_img * back_img + gate_txt * back_txt
    grad_pre = gelu_back(grad_hidden.reshape(pre.shape))[0]
    grad_log_gate = jnp.sum(hidden_rows * grad_hidden, axis=3).reshape(-1, 1)
    grad_row_logits = grad_log_gate * (my_expert - row_prob)
    grad_rows = mm_nt(grad_pre, w_in) + mm_nt(grad_row_logits, router_weight)
    grad_rows = lax.psum_scatter(grad_rows, "expert", scatter_dimension=0, tiled=True)
    grad_back = a2a(grad_rows.reshape(CAP, n_dp, width), "dp", 1).reshape(CAP * experts, width)
    grad_dispatch = mm(onehot, grad_back, highest)

    mean_usage = usage_all / count_sum[:, None]
    log_usage = jnp.log(mean_usage)
    entropy_terms = jnp.sum(mean_usage * log_usage, axis=1)
    usage_factor = entropy_weight * total_tokens * (log_usage + 1.0) / count_sum[:, None]
    grad_prob = mm_tn(modal_mask, usage_factor, highest)
    grad_logits = router_prob * (
        grad_prob - jnp.sum(router_prob * grad_prob, axis=1, keepdims=True)
    )

    grad_expert_in = mm_tn(rows, grad_pre)
    grad_expert_out = mm_nt(mm_tn(sum_img, grad_img), projection_img) + mm_nt(
        mm_tn(sum_txt, grad_txt), projection_txt
    )
    router_part = mm_tn(grad_row_logits, rows) + mm_tn(grad_logits, tokens)
    router_cut = jnp.sum(a2a(router_part, "dp", 0), axis=0, keepdims=True)
    router_cut = jnp.sum(gather(router_cut, "expert"), axis=0, keepdims=True)
    grad_router = gather(router_cut, "dp").T

    own = (lax.broadcasted_iota(jnp.int32, (1, pairs), 1) == own_pair).astype(jnp.float32)
    pooled_part = jnp.concatenate(
        [
            dot(w_out, sum_img, ((0,), (1,))) + token_means[0][:, None] * own,
            dot(w_out, sum_txt, ((0,), (1,))) + token_means[1][:, None] * own,
        ],
        axis=1,
    )
    pooled_cut = lax.psum_scatter(pooled_part, "expert", scatter_dimension=0, tiled=True)
    projection_part = jnp.concatenate(
        [mm(pooled_cut[:, :pairs], grad_img), mm(pooled_cut[:, pairs:], grad_txt)], axis=0
    )
    cut_rows = projection_part.shape[0] // n_dp
    projection_cut = jnp.sum(
        a2a(projection_part.reshape(n_dp, cut_rows, embed_width), "dp", 0), axis=0, keepdims=True
    )
    grad_projection = gather(projection_cut, "dp").reshape(projection.shape)

    own_img = lax.dynamic_slice_in_dim(grad_img, own_pair, 1, 0)
    own_txt = lax.dynamic_slice_in_dim(grad_txt, own_pair, 1, 0)
    grad_pooled = jnp.concatenate(
        [mm_nt(own_img, projection_img), mm_nt(own_txt, projection_txt)], axis=0
    )
    grad_output = mm_tn(modal_mask, grad_pooled / group_sizes[:, None], highest)
    grad_tokens = grad_output + mm_nt(grad_logits, router_weight, highest) + grad_dispatch
    losses = jnp.stack([contrast, entropy_terms[0], entropy_terms[1]])
    return (
        losses,
        grad_tokens,
        grad_router,
        grad_expert_in[None],
        grad_expert_out[None],
        grad_projection,
    )


def solution(mesh):
    return jax.shard_map(
        body,
        mesh=mesh,
        in_specs=(
            P(("dp", "expert"), None),
            P(),
            P("dp", None, "expert"),
            P("dp", "expert", None),
            P(None, "expert", None),
            P(("dp", "expert")),
            P(("dp", "expert")),
        ),
        out_specs=(
            P(),
            P(("dp", "expert"), None),
            P(),
            P("dp", None, "expert"),
            P("dp", "expert", None),
            P(None, "expert", None),
        ),
        check_vma=False,
    )
```

```python
import jax
import jax.numpy as jnp
from jax import lax
from jax.sharding import PartitionSpec as P

highest = lax.Precision.HIGHEST
high = lax.Precision.HIGH
contrast_scale = 10.0
entropy_weight = 0.5
norm_epsilon = 1e-06
CAP = 5


def gelu_exact(values):
    return jax.nn.gelu(values, approximate=False)


def dot(a, b, dims, precision=high):
    return lax.dot_general(a, b, (dims, ((), ())), precision=precision)


def mm(a, b, precision=high):
    return dot(a, b, ((1,), (0,)), precision)


def mm_nt(a, b, precision=high):
    return dot(a, b, ((1,), (1,)), precision)


def mm_tn(a, b, precision=high):
    return dot(a, b, ((0,), (0,)), precision)


def a2a(values, axis_name, axis):
    return lax.all_to_all(values, axis_name, split_axis=axis, concat_axis=axis, tiled=True)


def gather(values, axis_name):
    return lax.all_gather(values, axis_name, axis=0, tiled=True)


def after(values):
    return jnp.minimum(jnp.abs(values[(0,) * values.ndim]), 0.0)


def body(tokens, router_weight, expert_in, expert_out, projection, assignment, modality):
    tok_count, width = tokens.shape
    experts = router_weight.shape[1]
    n_dp = lax.axis_size("dp")
    n_z = lax.axis_size("expert")
    pairs = n_dp * n_z
    total_tokens = tok_count * pairs
    w_in = expert_in[0]
    w_out = expert_out[0]
    hidden_dev = w_in.shape[1]
    embed_width = projection.shape[2]
    my_dp = lax.axis_index("dp")
    my_z = lax.axis_index("expert")
    own_pair = my_z * n_dp + my_dp
    my_core = my_dp & 1

    def step(values, shift):
        return lax.ppermute(values, "expert", [(i, (i + shift) % n_z) for i in range(n_z)])

    projection_mine = gather(jnp.where(my_core == 0, projection[0], projection[1]), "expert")
    projection_other = lax.ppermute(projection_mine, "dp", [(i, i ^ 1) for i in range(n_dp)])

    expert_ids = lax.broadcasted_iota(jnp.int32, (1, experts), 1)
    chosen_mask = (assignment[:, None] == expert_ids).astype(jnp.float32)
    before = (
        lax.broadcasted_iota(jnp.int32, (tok_count, tok_count), 0)
        > lax.broadcasted_iota(jnp.int32, (tok_count, tok_count), 1)
    ).astype(jnp.bfloat16)
    earlier = jnp.dot(
        before, chosen_mask.astype(jnp.bfloat16), preferred_element_type=jnp.float32
    )
    slot = jnp.sum(earlier * chosen_mask, axis=1).astype(jnp.int32)
    cell_ids = lax.broadcasted_iota(jnp.int32, (1, CAP * experts), 1)
    onehot = ((slot * experts + assignment)[:, None] == cell_ids).astype(jnp.float32)
    dispatched = mm_tn(onehot, tokens, highest).reshape(CAP, experts, width)
    received = a2a(dispatched, "dp", 1).reshape(CAP * n_dp, width)

    projection_img = jnp.where(my_core == 0, projection_mine, projection_other)
    projection_txt = jnp.where(my_core == 0, projection_other, projection_mine)
    mixed_img = mm(w_out, projection_img)
    mixed_txt = mm(w_out, projection_txt)
    mixed_first = after(mixed_img) + after(mixed_txt)
    half = received.shape[0] // 2
    left1, right1 = lax.optimization_barrier((step(received, -1), step(received, 1)))
    left2, right2 = lax.optimization_barrier((step(left1, -1), step(right1, 1)))
    left3, right3 = lax.optimization_barrier((step(left2, -1), step(right2, 1)))
    middle = jnp.concatenate(
        [step(left3[:half] + mixed_first, -1), step(right3[half:] + mixed_first, 1)], axis=0
    )
    blocks = [received, left1, left2, left3, middle, right3, right2, right1]

    logits = mm(tokens, router_weight, highest)
    exponent = jnp.exp(logits)
    router_prob = exponent / jnp.sum(exponent, axis=1, keepdims=True)
    is_image = (modality == 0).astype(jnp.float32)
    modal_mask = jnp.stack([is_image, 1.0 - is_image], axis=0)
    images = jnp.sum(is_image)
    group_sizes = jnp.stack([images, tok_count - images])
    usage_part = mm(modal_mask, router_prob, highest).reshape(1, 2 * experts)
    image_slots = dot(chosen_mask, is_image, ((0,), (0,)), highest)
    meta = jnp.concatenate(
        [
            image_slots[:, None],
            jnp.broadcast_to(images, (experts, 1)),
            jnp.broadcast_to(usage_part, (experts, 2 * experts)),
            received[:experts, : 126 - 2 * experts],
        ],
        axis=1,
    )
    meta = a2a(meta, "dp", 0)
    meta = a2a(jnp.broadcast_to(meta[None], (n_z, n_dp, 128)), "expert", 0)
    meta_all = lax.dynamic_slice_in_dim(jnp.concatenate([meta, meta], axis=0), my_z, n_z, 0)
    token_means = mm(modal_mask / group_sizes[:, None], tokens, highest)

    embed_means = jnp.concatenate(
        [mm(token_means[:1], projection_img), mm(token_means[1:], projection_txt)], axis=0
    )

    usage_all = jnp.sum(meta[:, :, 2 : 2 + 2 * experts], axis=(0, 1)).reshape(2, experts)
    images_of = meta_all[:, :, 1]
    image_total = jnp.sum(meta[:, :, 1])
    count_sum = jnp.stack([image_total, total_tokens - image_total])
    slot_ids = lax.broadcasted_iota(jnp.int32, (1, CAP, 1), 1).astype(jnp.float32)
    in_image = slot_ids < meta_all[:, None, :, 0]
    weight_img = jnp.where(in_image, 1.0 / images_of[:, None], 0.0)
    weight_txt = jnp.where(in_image, 0.0, 1.0 / (tok_count - images_of)[:, None])

    w_cat = jnp.concatenate([w_in, router_weight], axis=1)
    my_expert = (expert_ids == my_dp).astype(jnp.float32)

    def forward_block(r):
        both = mm(blocks[r], w_cat)
        pre = both[:, :hidden_dev]
        row_exponent = jnp.exp(both[:, hidden_dev:])
        row_prob = row_exponent / jnp.sum(row_exponent, axis=1, keepdims=True)
        row_gate = jnp.sum(row_prob * my_expert, axis=1).reshape(CAP, n_dp)
        hidden = gelu_exact(pre).reshape(CAP, n_dp, hidden_dev)
        gate_img = (row_gate * weight_img[r])[..., None]
        gate_txt = (row_gate * weight_txt[r])[..., None]
        sum_img = jnp.sum(hidden * gate_img, axis=0)
        sum_txt = jnp.sum(hidden * gate_txt, axis=0)
        return pre, hidden, row_prob, gate_img, gate_txt, sum_img, sum_txt

    done = [forward_block(r) for r in range(n_z)]
    sum_img = jnp.stack([d[5] for d in done])
    sum_txt = jnp.stack([d[6] for d in done])

    part = jnp.stack(
        [
            mm(sum_img.reshape(pairs, hidden_dev), mixed_img).reshape(n_z, n_dp, embed_width),
            mm(sum_txt.reshape(pairs, hidden_dev), mixed_txt).reshape(n_z, n_dp, embed_width),
        ],
        axis=0,
    )
    part = part.transpose(2, 0, 1, 3).reshape(n_dp, 2 * n_z, embed_width)
    part = jnp.sum(a2a(part, "dp", 0), axis=0).reshape(2, n_z, embed_width)
    part = jnp.concatenate([part[:, :1] + embed_means[:, None], part[:, 1:]], axis=1)
    part = lax.dynamic_slice_in_dim(jnp.concatenate([part, part], axis=1), n_z - my_z, n_z, 1)
    part = a2a(jnp.broadcast_to(part[None], (n_z, 2, n_z, embed_width)), "expert", 0)
    column = jnp.sum(part, axis=0)
    every = a2a(
        jnp.broadcast_to(column.reshape(1, 2 * n_z, embed_width), (n_dp, 2 * n_z, embed_width)),
        "dp",
        0,
    )
    every = every.reshape(n_dp, 2, n_z, embed_width).transpose(1, 2, 0, 3)
    every = every.reshape(2, pairs, embed_width)

    def normalized(values):
        radius = jnp.sqrt(jnp.sum(values * values, axis=1, keepdims=True) + norm_epsilon)
        return values / radius, radius

    unit_img, radius_img = normalized(every[0])
    unit_txt, radius_txt = normalized(every[1])
    scores = contrast_scale * mm_nt(unit_img, unit_txt, highest)
    exp_scores = jnp.exp(scores)
    total_img = jnp.sum(exp_scores, axis=1, keepdims=True)
    total_txt = jnp.sum(exp_scores, axis=0, keepdims=True)
    diagonal = (
        lax.broadcasted_iota(jnp.int32, (pairs, pairs), 0)
        == lax.broadcasted_iota(jnp.int32, (pairs, pairs), 1)
    ).astype(jnp.float32)
    contrast = (
        jnp.sum(jnp.log(total_img)) + jnp.sum(jnp.log(total_txt)) - 2.0 * jnp.sum(scores * diagonal)
    ) / (2.0 * pairs)
    coupling = (exp_scores / total_img + exp_scores / total_txt - 2.0 * diagonal) * (
        contrast_scale * total_tokens / (2.0 * pairs)
    )

    def embed_back(unit, radius, grad_unit):
        return (grad_unit - unit * jnp.sum(unit * grad_unit, axis=1, keepdims=True)) / radius

    grad_img = embed_back(unit_img, radius_img, mm(coupling, unit_txt, highest))
    grad_txt = embed_back(unit_txt, radius_txt, mm_tn(coupling, unit_img, highest))

    back_img = mm_nt(grad_img, mixed_img).reshape(n_z, 1, n_dp, hidden_dev)
    back_txt = mm_nt(grad_txt, mixed_txt).reshape(n_z, 1, n_dp, hidden_dev)

    def backward_block(r):
        pre, hidden, row_prob, gate_img, gate_txt = done[r][:5]
        plane = (my_z + r) & (n_z - 1)
        grad_hidden = gate_img * lax.dynamic_index_in_dim(
            back_img, plane, 0, False
        ) + gate_txt * lax.dynamic_index_in_dim(back_txt, plane, 0, False)
        grad_pre = jax.vjp(gelu_exact, pre)[1](grad_hidden.reshape(pre.shape))[0]
        grad_log_gate = jnp.sum(hidden * grad_hidden, axis=2).reshape(-1, 1)
        grad_both = jnp.concatenate(
            [grad_pre, grad_log_gate * (my_expert - row_prob)], axis=1
        )
        return grad_both, lax.optimization_barrier(mm_nt(grad_both, w_cat))

    grads = [None] * n_z
    for r in (4, 3, 5, 2, 6, 1, 7, 0):
        grads[r] = backward_block(r)
    mean_usage = usage_all / count_sum[:, None]
    log_usage = jnp.log(mean_usage)
    entropy_terms = jnp.sum(mean_usage * log_usage, axis=1)
    usage_factor = entropy_weight * total_tokens * (log_usage + 1.0) / count_sum[:, None]
    grad_prob = mm_tn(modal_mask, usage_factor, highest)
    grad_logits = router_prob * (
        grad_prob - jnp.sum(router_prob * grad_prob, axis=1, keepdims=True)
    )

    sums = jnp.stack([sum_img, sum_txt])
    sums = lax.dynamic_slice_in_dim(jnp.concatenate([sums, sums], axis=1), n_z - my_z, n_z, 1)
    sums = sums.reshape(2 * pairs, hidden_dev)
    column_ids = lax.broadcasted_iota(jnp.int32, (1, 2 * pairs), 1)
    pooled_part = (
        dot(w_out, sums, ((0,), (1,)))
        + jnp.where(column_ids == own_pair, token_means[0][:, None], 0.0)
        + jnp.where(column_ids == own_pair + pairs, token_means[1][:, None], 0.0)
    )
    pooled_cut = lax.psum_scatter(pooled_part, "expert", scatter_dimension=0, tiled=True)
    projection_part = jnp.concatenate(
        [mm(pooled_cut[:, :pairs], grad_img), mm(pooled_cut[:, pairs:], grad_txt)], axis=0
    )
    cut = projection_part.shape[0] // n_dp
    rows = jnp.concatenate(blocks, axis=0)
    row_logits = jnp.concatenate([g[0][:, hidden_dev:] for g in grads], axis=0)
    router_part = mm_tn(row_logits, rows) + mm_tn(grad_logits, tokens)
    cut_router = -(-width // embed_width)
    router_part = jnp.pad(router_part, ((0, 0), (0, cut_router * embed_width - width)))
    shared = jnp.concatenate(
        [
            projection_part.reshape(n_dp, cut, embed_width),
            router_part.reshape(n_dp, cut_router, embed_width),
        ],
        axis=1,
    )
    shared = jnp.sum(a2a(shared, "dp", 0), axis=0)
    shared_first = after(shared)
    router_cut = a2a(
        jnp.broadcast_to(shared[None, cut:], (n_z, cut_router, embed_width)), "expert", 0
    )
    shared = jnp.concatenate([shared[:cut], jnp.sum(router_cut, axis=0)], axis=0)
    shared = a2a(jnp.broadcast_to(shared[None], (n_dp,) + shared.shape), "dp", 0)
    all_first = after(shared)
    grad_projection = shared[:, :cut].reshape(projection.shape)
    grad_router = shared[:, cut:].reshape(n_dp, cut_router * embed_width)[:, :width].T

    grad_expert_in = mm_tn(rows, jnp.concatenate([g[0][:, :hidden_dev] for g in grads], axis=0))
    transfer_img = mm_tn(sums[:pairs], grad_img)
    transfer_txt = mm_tn(sums[pairs:], grad_txt)
    grad_expert_out = mm_nt(transfer_img, projection_img) + mm_nt(transfer_txt, projection_txt)

    farthest = grads[4][1]
    ahead, behind = lax.optimization_barrier((step(farthest[half:], 1), step(farthest[:half], -1)))
    ahead, behind = lax.optimization_barrier(
        (
            step(jnp.concatenate([grads[3][1][:half], grads[3][1][half:] + ahead], axis=0), 1),
            step(jnp.concatenate([grads[5][1][:half] + behind, grads[5][1][half:]], axis=0), -1),
        )
    )
    ahead, behind = lax.optimization_barrier(
        (step(grads[2][1] + ahead, 1), step(grads[6][1] + behind, -1))
    )
    ahead, behind = lax.optimization_barrier(
        (
            step(grads[1][1] + ahead + shared_first, 1),
            step(grads[7][1] + behind + shared_first, -1),
        )
    )
    grad_rows = grads[0][1] + ahead + behind + all_first
    grad_back = a2a(grad_rows.reshape(CAP, n_dp, width), "dp", 1).reshape(CAP * experts, width)
    grad_dispatch = mm(onehot, grad_back, highest)

    own_img = lax.dynamic_slice_in_dim(grad_img, own_pair, 1, 0)
    own_txt = lax.dynamic_slice_in_dim(grad_txt, own_pair, 1, 0)
    grad_pooled = jnp.concatenate(
        [mm_nt(own_img, projection_img), mm_nt(own_txt, projection_txt)], axis=0
    )
    grad_output = mm_tn(modal_mask, grad_pooled / group_sizes[:, None], highest)
    grad_tokens = grad_output + mm_nt(grad_logits, router_weight, highest) + grad_dispatch
    losses = jnp.stack([contrast, entropy_terms[0], entropy_terms[1]])
    return (
        losses,
        grad_tokens,
        grad_router,
        grad_expert_in[None],
        grad_expert_out[None],
        grad_projection,
    )


def solution(mesh):
    return jax.shard_map(
        body,
        mesh=mesh,
        in_specs=(
            P(("dp", "expert"), None),
            P(),
            P("dp", None, "expert"),
            P("dp", "expert", None),
            P(None, "expert", None),
            P(("dp", "expert")),
            P(("dp", "expert")),
        ),
        out_specs=(
            P(),
            P(("dp", "expert"), None),
            P(),
            P("dp", None, "expert"),
            P("dp", "expert", None),
            P(None, "expert", None),
        ),
        check_vma=False,
    )
```

```python
import functools
import math

import jax
import jax.numpy as jnp
from jax import lax
from jax.experimental import pallas as pl
from jax.experimental.pallas import tpu as pltpu
from jax.sharding import PartitionSpec as P

highest = lax.Precision.HIGHEST
high = lax.Precision.HIGH
contrast_scale = 10.0
entropy_weight = 0.5
norm_epsilon = 1e-06
CAP = 5
PAIR_LEN = 128


def gelu_exact(values):
    return jax.nn.gelu(values, approximate=False)


def dot(a, b, dims, precision=high):
    return lax.dot_general(a, b, (dims, ((), ())), precision=precision)


def mm(a, b, precision=high):
    return dot(a, b, ((1,), (0,)), precision)


def mm_nt(a, b, precision=high):
    return dot(a, b, ((1,), (1,)), precision)


def mm_tn(a, b, precision=high):
    return dot(a, b, ((0,), (0,)), precision)


def a2a(values, axis_name, axis):
    return lax.all_to_all(values, axis_name, split_axis=axis, concat_axis=axis, tiled=True)


def gather(values, axis_name):
    return lax.all_gather(values, axis_name, axis=0, tiled=True)


def after(values):
    return jnp.minimum(jnp.abs(values[(0,) * values.ndim]), 0.0)


def halves(values):
    large = values.astype(jnp.bfloat16)
    return large, (values - large.astype(jnp.float32)).astype(jnp.bfloat16)


def weight_halves(values):
    large = lax.reduce_precision(values, exponent_bits=8, mantissa_bits=7)
    return large.astype(jnp.bfloat16), (values - large).astype(jnp.bfloat16)


def dot3(a, b, dims):
    def one(x, y):
        return lax.dot_general(x, y, (dims, ((), ())), preferred_element_type=jnp.float32)

    return one(a[0], b[0]) + (one(a[0], b[1]) + one(a[1], b[0]))


def call(kernel, shapes, args, scratch=(), mib=24, flops=0):
    vmem = pl.BlockSpec(memory_space=pltpu.VMEM)
    moved = sum(a.size * a.dtype.itemsize for a in args[1:]) + sum(
        4 * math.prod(shape) for shape in shapes
    )
    return pl.pallas_call(
        kernel,
        out_shape=[jax.ShapeDtypeStruct(shape, jnp.float32) for shape in shapes],
        in_specs=[pl.BlockSpec(memory_space=pltpu.SMEM)] + [vmem] * (len(args) - 1),
        out_specs=[vmem] * len(shapes),
        scratch_shapes=list(scratch),
        compiler_params=pltpu.CompilerParams(vmem_limit_bytes=mib << 20),
        cost_estimate=pl.CostEstimate(flops=flops, bytes_accessed=moved, transcendentals=0),
    )(*args)


LANES = 128
NN = ((1,), (0,))
NT = ((1,), (1,))
TN = ((0,), (0,))


def forward_kernel(experts, where, rows, w_large, w_small, gated, slope, prob):
    both = dot3(halves(rows[...]), (w_large[...], w_small[...]), NN)
    lane = lax.broadcasted_iota(jnp.int32, (both.shape[0], LANES), 1)
    exponent = jnp.where(lane < experts, jnp.exp(both[:, :LANES]), 0.0)
    probs = exponent / jnp.sum(exponent, axis=1, keepdims=True)
    prob[...] = probs
    gate = jnp.sum(jnp.where(lane == where[1], probs, 0.0), axis=1, keepdims=True)
    pre = both[:, LANES:]
    normal = 0.5 * (1.0 + lax.erf(pre * math.sqrt(0.5)))
    gated[...] = gate * (pre * normal)
    density = jnp.exp(-0.5 * pre * pre) * (1.0 / math.sqrt(2.0 * math.pi))
    slope[...] = gate * (normal + pre * density)


def slot_weights(meta, slot):
    in_image = slot < meta[:, 0:1]
    images = meta[:, 1:2]
    return (
        jnp.where(in_image, 1.0 / images, 0.0),
        jnp.where(in_image, 0.0, 1.0 / (PAIR_LEN - images)),
    )


def embed_kernel(n_z, n_dp, where, *refs):
    gated = refs[:n_z]
    meta, m_large, m_small, part, sums = refs[n_z:]
    for r in range(n_z):
        plane = (where[0] + r) & (n_z - 1)
        block = meta[plane]
        image = text = 0.0
        for slot in range(CAP):
            weight_img, weight_txt = slot_weights(block, float(slot))
            rows = gated[r][slot * n_dp : (slot + 1) * n_dp, :]
            image = image + weight_img * rows
            text = text + weight_txt * rows
        sums[0, :, pl.ds(plane, 1), :] = image[:, None]
        sums[1, :, pl.ds(plane, 1), :] = text[:, None]
    for m in range(2):
        rows = sums[m].reshape(n_dp * n_z, sums.shape[3])
        embed = dot3(halves(rows), (m_large[m], m_small[m]), NN)
        part[:, m * n_z : (m + 1) * n_z, :] = embed.reshape(n_dp, n_z, embed.shape[1])


def head_kernel(n_z, factor, where, every, m_large, m_small, grads, back, contrast):
    pairs = every.shape[0] * n_z
    width = every.shape[2]

    def unit_of(m):
        values = every[:, m * n_z : (m + 1) * n_z, :].reshape(pairs, width)
        radius = jnp.sqrt(jnp.sum(values * values, axis=1, keepdims=True) + norm_epsilon)
        return values / radius, radius

    def product(a, b, dims):
        return lax.dot_general(a, b, (dims, ((), ())), precision=highest)

    unit_img, radius_img = unit_of(0)
    unit_txt, radius_txt = unit_of(1)
    scores = contrast_scale * product(unit_img, unit_txt, NT)
    exp_scores = jnp.exp(scores)
    total_img = jnp.sum(exp_scores, axis=1, keepdims=True)
    total_txt = jnp.sum(exp_scores, axis=0, keepdims=True)
    shape = (pairs, pairs)
    same = lax.broadcasted_iota(jnp.int32, shape, 0) == lax.broadcasted_iota(jnp.int32, shape, 1)
    logs = (
        jnp.sum(jnp.log(total_img), axis=0, keepdims=True)
        + jnp.sum(jnp.log(total_txt), axis=1, keepdims=True)
    )
    matched = jnp.sum(jnp.where(same, scores, 0.0), axis=1, keepdims=True)
    matched = jnp.sum(matched, axis=0, keepdims=True)
    contrast[...] = jnp.broadcast_to((logs - 2.0 * matched) / (2.0 * pairs), contrast.shape)
    coupling = (
        exp_scores / total_img + exp_scores / total_txt - jnp.where(same, 2.0, 0.0)
    ) * factor
    for m, unit, radius, grad_unit in (
        (0, unit_img, radius_img, product(coupling, unit_txt, NN)),
        (1, unit_txt, radius_txt, product(coupling.T, unit_img, NN)),
    ):
        along = jnp.sum(unit * grad_unit, axis=1, keepdims=True)
        grad = (grad_unit - unit * along) / radius
        grads[m] = grad
        q = dot3(halves(grad), (m_large[m], m_small[m]), NT)
        back[m] = q.reshape(every.shape[0], n_z, q.shape[1])


def backward_kernel(
    n_z, n_dp, r, where, rows, gated, slope, prob, meta, back, w_large, w_small, router_in,
    both, grad_rows, router_out,
):
    plane = (where[0] + r) & (n_z - 1)
    back_img = back[0, :, pl.ds(plane, 1), :].reshape(n_dp, back.shape[3])
    back_txt = back[1, :, pl.ds(plane, 1), :].reshape(n_dp, back.shape[3])
    block = meta[plane]
    lane = lax.broadcasted_iota(jnp.int32, (n_dp, LANES), 1)
    for slot in range(CAP):
        part = slice(slot * n_dp, (slot + 1) * n_dp)
        weight_img, weight_txt = slot_weights(block, float(slot))
        mixed = weight_img * back_img + weight_txt * back_txt
        both[part, LANES:] = slope[part, :] * mixed
        log_gate = jnp.sum(gated[part, :] * mixed, axis=1, keepdims=True)
        chosen = jnp.where(lane == where[1], 1.0, 0.0)
        both[part, :LANES] = log_gate * (chosen - prob[part, :])
    pair = halves(both[...])
    grad_rows[...] = dot3(pair, (w_large[...], w_small[...]), NT)
    logits = (pair[0][:, :LANES], pair[1][:, :LANES])
    router_out[...] = router_in[...] + dot3(logits, halves(rows[...]), TN)


def body(tokens, router_weight, expert_in, expert_out, projection, assignment, modality):
    tok_count, width = tokens.shape
    experts = router_weight.shape[1]
    n_dp = lax.axis_size("dp")
    n_z = lax.axis_size("expert")
    pairs = n_dp * n_z
    total_tokens = tok_count * pairs
    w_in = expert_in[0]
    w_out = expert_out[0]
    hidden_dev = w_in.shape[1]
    embed_width = projection.shape[2]
    my_dp = lax.axis_index("dp")
    my_z = lax.axis_index("expert")
    own_pair = my_dp * n_z + my_z
    where = jnp.stack([my_z, my_dp])
    my_core = my_dp & 1

    def step(values, shift):
        return lax.ppermute(values, "expert", [(i, (i + shift) % n_z) for i in range(n_z)])

    projection_mine = gather(jnp.where(my_core == 0, projection[0], projection[1]), "expert")
    projection_other = lax.ppermute(projection_mine, "dp", [(i, i ^ 1) for i in range(n_dp)])

    expert_ids = lax.broadcasted_iota(jnp.int32, (1, experts), 1)
    chosen_mask = (assignment[:, None] == expert_ids).astype(jnp.float32)
    before = (
        lax.broadcasted_iota(jnp.int32, (tok_count, tok_count), 0)
        > lax.broadcasted_iota(jnp.int32, (tok_count, tok_count), 1)
    ).astype(jnp.bfloat16)
    earlier = jnp.dot(
        before, chosen_mask.astype(jnp.bfloat16), preferred_element_type=jnp.float32
    )
    slot = jnp.sum(earlier * chosen_mask, axis=1).astype(jnp.int32)
    cell_ids = lax.broadcasted_iota(jnp.int32, (1, CAP * experts), 1)
    onehot = ((slot * experts + assignment)[:, None] == cell_ids).astype(jnp.float32)
    dispatched = mm_tn(onehot, tokens, highest).reshape(CAP, experts, width)
    received = a2a(dispatched, "dp", 1).reshape(CAP * n_dp, width)

    projection_img = jnp.where(my_core == 0, projection_mine, projection_other)
    projection_txt = jnp.where(my_core == 0, projection_other, projection_mine)
    mixed_img = mm(w_out, projection_img)
    mixed_txt = mm(w_out, projection_txt)
    mixed_first = after(mixed_img) + after(mixed_txt)
    half = received.shape[0] // 2
    left1, right1 = lax.optimization_barrier((step(received, -1), step(received, 1)))
    left2, right2 = lax.optimization_barrier((step(left1, -1), step(right1, 1)))
    left3, right3 = lax.optimization_barrier((step(left2, -1), step(right2, 1)))
    middle = jnp.concatenate(
        [step(left3[:half] + mixed_first, -1), step(right3[half:] + mixed_first, 1)], axis=0
    )
    blocks = [received, left1, left2, left3, middle, right3, right2, right1]

    logits = mm(tokens, router_weight, highest)
    exponent = jnp.exp(logits)
    router_prob = exponent / jnp.sum(exponent, axis=1, keepdims=True)
    is_image = (modality == 0).astype(jnp.float32)
    modal_mask = jnp.stack([is_image, 1.0 - is_image], axis=0)
    images = jnp.sum(is_image)
    group_sizes = jnp.stack([images, tok_count - images])
    usage_part = mm(modal_mask, router_prob, highest).reshape(1, 2 * experts)
    image_slots = dot(chosen_mask, is_image, ((0,), (0,)), highest)
    meta = jnp.concatenate(
        [
            image_slots[:, None],
            jnp.broadcast_to(images, (experts, 1)),
            jnp.broadcast_to(usage_part, (experts, 2 * experts)),
            received[:experts, : 126 - 2 * experts],
        ],
        axis=1,
    )
    meta = a2a(meta, "dp", 0)
    meta = a2a(jnp.broadcast_to(meta[None], (n_z, n_dp, 128)), "expert", 0)
    token_means = mm(modal_mask / group_sizes[:, None], tokens, highest)

    embed_means = jnp.concatenate(
        [mm(token_means[:1], projection_img), mm(token_means[1:], projection_txt)], axis=0
    )

    usage_all = jnp.sum(meta[:, :, 2 : 2 + 2 * experts], axis=(0, 1)).reshape(2, experts)
    image_total = jnp.sum(meta[:, :, 1])
    count_sum = jnp.stack([image_total, total_tokens - image_total])

    slots = CAP * n_dp
    w_pair = weight_halves(
        jnp.concatenate(
            [jnp.pad(router_weight, ((0, 0), (0, LANES - experts))), w_in], axis=1
        )
    )
    wide = LANES + hidden_dev
    done = [
        call(
            functools.partial(forward_kernel, experts),
            [(slots, hidden_dev), (slots, hidden_dev), (slots, LANES)],
            (where, blocks[r], *w_pair),
            flops=6 * slots * width * wide,
        )
        for r in range(n_z)
    ]

    mixed_pair = weight_halves(jnp.stack([mixed_img, mixed_txt]))
    part, sums = call(
        functools.partial(embed_kernel, n_z, n_dp),
        [(n_dp, 2 * n_z, embed_width), (2, n_dp, n_z, hidden_dev)],
        (where, *[d[0] for d in done], meta, *mixed_pair),
        flops=12 * pairs * hidden_dev * embed_width,
    )
    part = jnp.sum(a2a(part, "dp", 0), axis=0).reshape(2, n_z, embed_width)
    own_plane = lax.broadcasted_iota(jnp.int32, (1, n_z, 1), 1) == my_z
    part = part + jnp.where(own_plane, embed_means[:, None], 0.0)
    part = a2a(jnp.broadcast_to(part[None], (n_z, 2, n_z, embed_width)), "expert", 0)
    column = jnp.sum(part, axis=0).reshape(1, 2 * n_z, embed_width)
    every = a2a(jnp.broadcast_to(column, (n_dp, 2 * n_z, embed_width)), "dp", 0)
    pair_grads, back, contrast = call(
        functools.partial(
            head_kernel, n_z, contrast_scale * total_tokens / (2.0 * pairs)
        ),
        [(2, pairs, embed_width), (2, n_dp, n_z, hidden_dev), (8, LANES)],
        (where, every, *mixed_pair),
        mib=40,
        flops=36 * pairs * pairs * embed_width + 12 * pairs * hidden_dev * embed_width,
    )
    grad_img, grad_txt = pair_grads[0], pair_grads[1]
    contrast = contrast[0, 0]

    grads = [None] * n_z
    router_sum = jnp.zeros((LANES, width), jnp.float32)
    for r in (4, 3, 5, 2, 6, 1, 7, 0):
        both, back_rows, router_sum = call(
            functools.partial(backward_kernel, n_z, n_dp, r),
            [(slots, wide), (slots, width), (LANES, width)],
            (where, blocks[r], *done[r], meta, back, *w_pair, router_sum),
            flops=6 * slots * width * (wide + LANES),
        )
        grads[r] = (both, back_rows)

    mean_usage = usage_all / count_sum[:, None]
    log_usage = jnp.log(mean_usage)
    entropy_terms = jnp.sum(mean_usage * log_usage, axis=1)
    usage_factor = entropy_weight * total_tokens * (log_usage + 1.0) / count_sum[:, None]
    grad_prob = mm_tn(modal_mask, usage_factor, highest)
    grad_logits = router_prob * (
        grad_prob - jnp.sum(router_prob * grad_prob, axis=1, keepdims=True)
    )

    sums = sums.reshape(2 * pairs, hidden_dev)
    column_ids = lax.broadcasted_iota(jnp.int32, (1, 2 * pairs), 1)
    pooled_part = (
        dot(w_out, sums, ((0,), (1,)))
        + jnp.where(column_ids == own_pair, token_means[0][:, None], 0.0)
        + jnp.where(column_ids == own_pair + pairs, token_means[1][:, None], 0.0)
    )
    pooled_cut = lax.psum_scatter(pooled_part, "expert", scatter_dimension=0, tiled=True)
    projection_part = jnp.concatenate(
        [mm(pooled_cut[:, :pairs], grad_img), mm(pooled_cut[:, pairs:], grad_txt)], axis=0
    )
    cut = projection_part.shape[0] // n_dp
    rows = jnp.concatenate(blocks, axis=0)
    router_part = router_sum[:experts] + mm_tn(grad_logits, tokens)
    cut_router = -(-width // embed_width)
    router_part = jnp.pad(router_part, ((0, 0), (0, cut_router * embed_width - width)))
    shared = jnp.concatenate(
        [
            projection_part.reshape(n_dp, cut, embed_width),
            router_part.reshape(n_dp, cut_router, embed_width),
        ],
        axis=1,
    )
    shared = jnp.sum(a2a(shared, "dp", 0), axis=0)
    shared_first = after(shared)
    router_cut = a2a(
        jnp.broadcast_to(shared[None, cut:], (n_z, cut_router, embed_width)), "expert", 0
    )
    shared = jnp.concatenate([shared[:cut], jnp.sum(router_cut, axis=0)], axis=0)
    shared = a2a(jnp.broadcast_to(shared[None], (n_dp,) + shared.shape), "dp", 0)
    all_first = after(shared)
    grad_projection = shared[:, :cut].reshape(projection.shape)
    grad_router = shared[:, cut:].reshape(n_dp, cut_router * embed_width)[:, :width].T

    grad_expert_in = mm_tn(rows, jnp.concatenate([g[0][:, LANES:] for g in grads], axis=0))
    transfer_img = mm_tn(sums[:pairs], grad_img)
    transfer_txt = mm_tn(sums[pairs:], grad_txt)
    grad_expert_out = mm_nt(transfer_img, projection_img) + mm_nt(transfer_txt, projection_txt)

    farthest = grads[4][1]
    ahead, behind = lax.optimization_barrier((step(farthest[half:], 1), step(farthest[:half], -1)))
    ahead, behind = lax.optimization_barrier(
        (
            step(jnp.concatenate([grads[3][1][:half], grads[3][1][half:] + ahead], axis=0), 1),
            step(jnp.concatenate([grads[5][1][:half] + behind, grads[5][1][half:]], axis=0), -1),
        )
    )
    ahead, behind = lax.optimization_barrier(
        (step(grads[2][1] + ahead, 1), step(grads[6][1] + behind, -1))
    )
    ahead, behind = lax.optimization_barrier(
        (
            step(grads[1][1] + ahead + shared_first, 1),
            step(grads[7][1] + behind + shared_first, -1),
        )
    )
    grad_rows = grads[0][1] + ahead + behind + all_first
    grad_back = a2a(grad_rows.reshape(CAP, n_dp, width), "dp", 1).reshape(CAP * experts, width)
    grad_dispatch = mm(onehot, grad_back, highest)

    own_img = lax.dynamic_slice_in_dim(grad_img, own_pair, 1, 0)
    own_txt = lax.dynamic_slice_in_dim(grad_txt, own_pair, 1, 0)
    grad_pooled = jnp.concatenate(
        [mm_nt(own_img, projection_img), mm_nt(own_txt, projection_txt)], axis=0
    )
    grad_output = mm_tn(modal_mask, grad_pooled / group_sizes[:, None], highest)
    grad_tokens = grad_output + mm_nt(grad_logits, router_weight, highest) + grad_dispatch
    losses = jnp.stack([contrast, entropy_terms[0], entropy_terms[1]])
    return (
        losses,
        grad_tokens,
        grad_router,
        grad_expert_in[None],
        grad_expert_out[None],
        grad_projection,
    )


def solution(mesh):
    return jax.shard_map(
        body,
        mesh=mesh,
        in_specs=(
            P(("dp", "expert"), None),
            P(),
            P("dp", None, "expert"),
            P("dp", "expert", None),
            P(None, "expert", None),
            P(("dp", "expert")),
            P(("dp", "expert")),
        ),
        out_specs=(
            P(),
            P(("dp", "expert"), None),
            P(),
            P("dp", None, "expert"),
            P("dp", "expert", None),
            P(None, "expert", None),
        ),
        check_vma=False,
    )
```

```python
import functools
import math

import jax
import jax.numpy as jnp
from jax import lax
from jax.experimental import pallas as pl
from jax.experimental.pallas import tpu as pltpu
from jax.sharding import PartitionSpec as P

highest = lax.Precision.HIGHEST
high = lax.Precision.HIGH
contrast_scale = 10.0
entropy_weight = 0.5
norm_epsilon = 1e-06
CAP = 5
PAIR_LEN = 128


def gelu_exact(values):
    return jax.nn.gelu(values, approximate=False)


def dot(a, b, dims, precision=high):
    return lax.dot_general(a, b, (dims, ((), ())), precision=precision)


def mm(a, b, precision=high):
    return dot(a, b, ((1,), (0,)), precision)


def mm_nt(a, b, precision=high):
    return dot(a, b, ((1,), (1,)), precision)


def mm_tn(a, b, precision=high):
    return dot(a, b, ((0,), (0,)), precision)


def a2a(values, axis_name, axis):
    return lax.all_to_all(values, axis_name, split_axis=axis, concat_axis=axis, tiled=True)


def gather(values, axis_name):
    return lax.all_gather(values, axis_name, axis=0, tiled=True)


def after(values):
    return jnp.minimum(jnp.abs(values[(0,) * values.ndim]), 0.0)


def halves(values):
    large = values.astype(jnp.bfloat16)
    return large, (values - large.astype(jnp.float32)).astype(jnp.bfloat16)


def weight_halves(values):
    large = lax.reduce_precision(values, exponent_bits=8, mantissa_bits=7)
    return large.astype(jnp.bfloat16), (values - large).astype(jnp.bfloat16)


def dot3(a, b, dims):
    def one(x, y):
        return lax.dot_general(x, y, (dims, ((), ())), preferred_element_type=jnp.float32)

    return one(a[0], b[0]) + (one(a[0], b[1]) + one(a[1], b[0]))


def call(kernel, shapes, args, us, mib=16, fetch=False):
    def whole(shape):
        if fetch:
            return pl.BlockSpec(shape, lambda i: (0,) * len(shape))
        return pl.BlockSpec(memory_space=pltpu.VMEM)

    return pl.pallas_call(
        kernel,
        out_shape=[jax.ShapeDtypeStruct(shape, jnp.float32) for shape in shapes],
        grid=(1,) if fetch else (),
        in_specs=[pl.BlockSpec(memory_space=pltpu.SMEM)] + [whole(a.shape) for a in args[1:]],
        out_specs=[whole(shape) for shape in shapes],
        compiler_params=pltpu.CompilerParams(vmem_limit_bytes=mib << 20),
        cost_estimate=pl.CostEstimate(
            flops=int(us * 1.1e9), bytes_accessed=1 << 20, transcendentals=0
        ),
    )(*args)


LANES = 128
NN = ((1,), (0,))
NT = ((1,), (1,))
TN = ((0,), (0,))


def forward_kernel(experts, where, rows, w_large, w_small, gated, slope):
    both = dot3(halves(rows[...]), (w_large[...], w_small[...]), NT)
    lane = lax.broadcasted_iota(jnp.int32, (both.shape[0], LANES), 1)
    exponent = jnp.where(lane < experts, jnp.exp(both[:, :LANES]), 0.0)
    probs = exponent / jnp.sum(exponent, axis=1, keepdims=True)
    slope[:, :LANES] = probs
    gate = jnp.sum(jnp.where(lane == where[1], probs, 0.0), axis=1, keepdims=True)
    pre = both[:, LANES:]
    normal = 0.5 * (1.0 + lax.erf(pre * math.sqrt(0.5)))
    gated[...] = gate * (pre * normal)
    density = jnp.exp(-0.5 * pre * pre) * (1.0 / math.sqrt(2.0 * math.pi))
    slope[:, LANES:] = gate * (normal + pre * density)


def slot_weights(meta, slot):
    in_image = slot < meta[:, 0:1]
    images = meta[:, 1:2]
    return (
        jnp.where(in_image, 1.0 / images, 0.0),
        jnp.where(in_image, 0.0, 1.0 / (PAIR_LEN - images)),
    )


def embed_kernel(n_z, n_dp, where, *refs):
    gated = refs[:n_z]
    meta, m_large, m_small, part, sums = refs[n_z:]
    for r in range(n_z):
        plane = (where[0] + r) & (n_z - 1)
        block = meta[plane]
        image = text = 0.0
        for slot in range(CAP):
            weight_img, weight_txt = slot_weights(block, float(slot))
            rows = gated[r][slot * n_dp : (slot + 1) * n_dp, :]
            image = image + weight_img * rows
            text = text + weight_txt * rows
        sums[0, :, pl.ds(plane, 1), :] = image[:, None]
        sums[1, :, pl.ds(plane, 1), :] = text[:, None]
    for m in range(2):
        rows = sums[m].reshape(n_dp * n_z, sums.shape[3])
        embed = dot3(halves(rows), (m_large[m], m_small[m]), NN)
        part[:, m * n_z : (m + 1) * n_z, :] = embed.reshape(n_dp, n_z, embed.shape[1])


def head_kernel(n_z, factor, where, every, m_large, m_small, grads, back, contrast):
    pairs = every.shape[0] * n_z
    width = every.shape[2]

    def unit_of(m):
        values = every[:, m * n_z : (m + 1) * n_z, :].reshape(pairs, width)
        radius = jnp.sqrt(jnp.sum(values * values, axis=1, keepdims=True) + norm_epsilon)
        return values / radius, radius

    def product(a, b, dims):
        return lax.dot_general(a, b, (dims, ((), ())), precision=highest)

    unit_img, radius_img = unit_of(0)
    unit_txt, radius_txt = unit_of(1)
    scores = contrast_scale * product(unit_img, unit_txt, NT)
    exp_scores = jnp.exp(scores)
    total_img = jnp.sum(exp_scores, axis=1, keepdims=True)
    total_txt = jnp.sum(exp_scores, axis=0, keepdims=True)
    shape = (pairs, pairs)
    same = lax.broadcasted_iota(jnp.int32, shape, 0) == lax.broadcasted_iota(jnp.int32, shape, 1)
    logs = (
        jnp.sum(jnp.log(total_img), axis=0, keepdims=True)
        + jnp.sum(jnp.log(total_txt), axis=1, keepdims=True)
    )
    matched = jnp.sum(jnp.where(same, scores, 0.0), axis=1, keepdims=True)
    matched = jnp.sum(matched, axis=0, keepdims=True)
    contrast[...] = jnp.broadcast_to((logs - 2.0 * matched) / (2.0 * pairs), contrast.shape)
    coupling = (
        exp_scores / total_img + exp_scores / total_txt - jnp.where(same, 2.0, 0.0)
    ) * factor
    for m, unit, radius, grad_unit in (
        (0, unit_img, radius_img, product(coupling, unit_txt, NN)),
        (1, unit_txt, radius_txt, product(coupling.T, unit_img, NN)),
    ):
        along = jnp.sum(unit * grad_unit, axis=1, keepdims=True)
        grad = (grad_unit - unit * along) / radius
        grads[m] = grad
        q = dot3(halves(grad), (m_large[m], m_small[m]), NT)
        back[m] = q.reshape(every.shape[0], n_z, q.shape[1])


def backward_kernel(n_z, n_dp, where, *refs):
    gated, slope, blocks = refs[:n_z], refs[n_z : 2 * n_z], refs[2 * n_z : 3 * n_z]
    meta, back, both, router_out = refs[3 * n_z :]
    lane = lax.broadcasted_iota(jnp.int32, (n_dp, LANES), 1)
    chosen = jnp.where(lane == where[1], 1.0, 0.0)
    slots = CAP * n_dp
    for r in range(n_z):
        plane = (where[0] + r) & (n_z - 1)
        back_img = back[0, :, pl.ds(plane, 1), :].reshape(n_dp, back.shape[3])
        back_txt = back[1, :, pl.ds(plane, 1), :].reshape(n_dp, back.shape[3])
        block = meta[plane]
        for slot in range(CAP):
            part = slice(slot * n_dp, (slot + 1) * n_dp)
            out = slice(r * slots + slot * n_dp, r * slots + (slot + 1) * n_dp)
            weight_img, weight_txt = slot_weights(block, float(slot))
            mixed = weight_img * back_img + weight_txt * back_txt
            both[out, LANES:] = slope[r][part, LANES:] * mixed
            log_gate = jnp.sum(gated[r][part, :] * mixed, axis=1, keepdims=True)
            both[out, :LANES] = log_gate * (chosen - slope[r][part, :LANES])
    total = 0.0
    for r in range(n_z):
        logits = both[r * slots : (r + 1) * slots, :LANES]
        total = total + dot3(halves(logits), halves(blocks[r][...]), TN)
    router_out[...] = total


def rows_kernel(which, where, both, w_large, w_small, *grad_rows):
    slots = grad_rows[0].shape[0]
    for r, out in zip(which, grad_rows):
        values = halves(both[r * slots : (r + 1) * slots, :])
        out[...] = dot3(values, (w_large[...], w_small[...]), NN)


def weight_kernel(where, both, *refs):
    blocks, out = refs[:-1], refs[-1]
    slots = blocks[0].shape[0]
    for r, rows in enumerate(blocks):
        values = halves(both[r * slots : (r + 1) * slots, LANES:])
        term = dot3(values, halves(rows[...]), TN)
        if r == 0:
            out[...] = term
        else:
            out[...] += term


def body(tokens, router_weight, expert_in, expert_out, projection, assignment, modality):
    tok_count, width = tokens.shape
    experts = router_weight.shape[1]
    n_dp = lax.axis_size("dp")
    n_z = lax.axis_size("expert")
    pairs = n_dp * n_z
    total_tokens = tok_count * pairs
    w_in = expert_in[0]
    w_out = expert_out[0]
    hidden_dev = w_in.shape[1]
    embed_width = projection.shape[2]
    my_dp = lax.axis_index("dp")
    my_z = lax.axis_index("expert")
    own_pair = my_dp * n_z + my_z
    where = jnp.stack([my_z, my_dp])
    my_core = my_dp & 1

    def step(values, shift):
        return lax.ppermute(values, "expert", [(i, (i + shift) % n_z) for i in range(n_z)])

    projection_mine = gather(jnp.where(my_core == 0, projection[0], projection[1]), "expert")
    projection_other = lax.ppermute(projection_mine, "dp", [(i, i ^ 1) for i in range(n_dp)])

    expert_ids = lax.broadcasted_iota(jnp.int32, (1, experts), 1)
    chosen_mask = (assignment[:, None] == expert_ids).astype(jnp.float32)
    before = (
        lax.broadcasted_iota(jnp.int32, (tok_count, tok_count), 0)
        > lax.broadcasted_iota(jnp.int32, (tok_count, tok_count), 1)
    ).astype(jnp.bfloat16)
    earlier = jnp.dot(
        before, chosen_mask.astype(jnp.bfloat16), preferred_element_type=jnp.float32
    )
    slot = jnp.sum(earlier * chosen_mask, axis=1).astype(jnp.int32)
    cell_ids = lax.broadcasted_iota(jnp.int32, (1, CAP * experts), 1)
    onehot = ((slot * experts + assignment)[:, None] == cell_ids).astype(jnp.float32)
    dispatched = mm_tn(onehot, tokens, highest).reshape(CAP, experts, width)
    received = a2a(dispatched, "dp", 1).reshape(CAP * n_dp, width)

    projection_img = jnp.where(my_core == 0, projection_mine, projection_other)
    projection_txt = jnp.where(my_core == 0, projection_other, projection_mine)
    mixed_img = mm(w_out, projection_img)
    mixed_txt = mm(w_out, projection_txt)
    mixed_first = after(mixed_img) + after(mixed_txt)
    half = received.shape[0] // 2
    left1, right1 = lax.optimization_barrier((step(received, -1), step(received, 1)))
    left2, right2 = lax.optimization_barrier((step(left1, -1), step(right1, 1)))
    left3, right3 = lax.optimization_barrier((step(left2, -1), step(right2, 1)))
    middle = jnp.concatenate(
        [step(left3[:half] + mixed_first, -1), step(right3[half:] + mixed_first, 1)], axis=0
    )
    blocks = [received, left1, left2, left3, middle, right3, right2, right1]

    logits = mm(tokens, router_weight, highest)
    exponent = jnp.exp(logits)
    router_prob = exponent / jnp.sum(exponent, axis=1, keepdims=True)
    is_image = (modality == 0).astype(jnp.float32)
    modal_mask = jnp.stack([is_image, 1.0 - is_image], axis=0)
    images = jnp.sum(is_image)
    group_sizes = jnp.stack([images, tok_count - images])
    usage_part = mm(modal_mask, router_prob, highest).reshape(1, 2 * experts)
    image_slots = dot(chosen_mask, is_image, ((0,), (0,)), highest)
    meta = jnp.concatenate(
        [
            image_slots[:, None],
            jnp.broadcast_to(images, (experts, 1)),
            jnp.broadcast_to(usage_part, (experts, 2 * experts)),
            received[:experts, : 126 - 2 * experts],
        ],
        axis=1,
    )
    meta = a2a(meta, "dp", 0)
    meta = a2a(jnp.broadcast_to(meta[None], (n_z, n_dp, 128)), "expert", 0)
    token_means = mm(modal_mask / group_sizes[:, None], tokens, highest)

    embed_means = jnp.concatenate(
        [mm(token_means[:1], projection_img), mm(token_means[1:], projection_txt)], axis=0
    )

    usage_all = jnp.sum(meta[:, :, 2 : 2 + 2 * experts], axis=(0, 1)).reshape(2, experts)
    image_total = jnp.sum(meta[:, :, 1])
    count_sum = jnp.stack([image_total, total_tokens - image_total])

    slots = CAP * n_dp
    w_pair = weight_halves(
        jnp.concatenate(
            [jnp.pad(router_weight.T, ((0, LANES - experts), (0, 0))), w_in.T], axis=0
        )
    )
    wide = LANES + hidden_dev
    done = [
        call(
            functools.partial(forward_kernel, experts),
            [(slots, hidden_dev), (slots, wide)],
            (where, blocks[r], *w_pair),
            us=2.5,
        )
        for r in range(n_z)
    ]

    mixed_pair = weight_halves(jnp.stack([mixed_img, mixed_txt]))
    part, sums = call(
        functools.partial(embed_kernel, n_z, n_dp),
        [(n_dp, 2 * n_z, embed_width), (2, n_dp, n_z, hidden_dev)],
        (where, *[d[0] for d in done], meta, *mixed_pair),
        us=3,
        mib=58,
        fetch=True,
    )
    sums = sums.reshape(2 * pairs, hidden_dev)
    column_ids = lax.broadcasted_iota(jnp.int32, (1, 2 * pairs), 1)
    pooled_part = (
        dot(w_out, sums, ((0,), (1,)))
        + jnp.where(column_ids == own_pair, token_means[0][:, None], 0.0)
        + jnp.where(column_ids == own_pair + pairs, token_means[1][:, None], 0.0)
    )
    pooled_cut = lax.psum_scatter(pooled_part, "expert", scatter_dimension=0, tiled=True)
    pooled_first = after(pooled_part)
    part = jnp.sum(a2a(part, "dp", 0), axis=0).reshape(2, n_z, embed_width)
    own_plane = lax.broadcasted_iota(jnp.int32, (1, n_z, 1), 1) == my_z
    part = part + jnp.where(own_plane, embed_means[:, None], 0.0) + pooled_first
    part = a2a(jnp.broadcast_to(part[None], (n_z, 2, n_z, embed_width)), "expert", 0)
    column = jnp.sum(part, axis=0).reshape(1, 2 * n_z, embed_width)
    every = a2a(jnp.broadcast_to(column, (n_dp, 2 * n_z, embed_width)), "dp", 0)
    pair_grads, back, contrast = call(
        functools.partial(
            head_kernel, n_z, contrast_scale * total_tokens / (2.0 * pairs)
        ),
        [(2, pairs, embed_width), (2, n_dp, n_z, hidden_dev), (8, LANES)],
        (where, every, *mixed_pair),
        us=5,
        mib=24,
    )
    grad_img, grad_txt = pair_grads[0], pair_grads[1]
    contrast = contrast[0, 0]

    both, router_sum = call(
        functools.partial(backward_kernel, n_z, n_dp),
        [(n_z * slots, wide), (LANES, width)],
        (where, *[d[0] for d in done], *[d[1] for d in done], *blocks, meta, back),
        us=8,
        mib=58,
        fetch=True,
    )
    grads = {}
    for which in ((4,), (3, 5), (2, 6), (1, 7, 0)):
        made = call(
            functools.partial(rows_kernel, which),
            [(slots, width)] * len(which),
            (where, both, *w_pair),
            us=1.8 * len(which),
        )
        grads.update(zip(which, made))

    mean_usage = usage_all / count_sum[:, None]
    log_usage = jnp.log(mean_usage)
    entropy_terms = jnp.sum(mean_usage * log_usage, axis=1)
    usage_factor = entropy_weight * total_tokens * (log_usage + 1.0) / count_sum[:, None]
    grad_prob = mm_tn(modal_mask, usage_factor, highest)
    grad_logits = router_prob * (
        grad_prob - jnp.sum(router_prob * grad_prob, axis=1, keepdims=True)
    )

    projection_part = jnp.concatenate(
        [mm(pooled_cut[:, :pairs], grad_img), mm(pooled_cut[:, pairs:], grad_txt)], axis=0
    )
    cut = projection_part.shape[0] // n_dp
    router_part = router_sum[:experts] + mm_tn(grad_logits, tokens)
    cut_router = -(-width // embed_width)
    router_part = jnp.pad(router_part, ((0, 0), (0, cut_router * embed_width - width)))
    shared = jnp.concatenate(
        [
            projection_part.reshape(n_dp, cut, embed_width),
            router_part.reshape(n_dp, cut_router, embed_width),
        ],
        axis=1,
    )
    shared = jnp.sum(a2a(shared, "dp", 0), axis=0)
    shared_first = after(shared)
    router_cut = a2a(
        jnp.broadcast_to(shared[None, cut:], (n_z, cut_router, embed_width)), "expert", 0
    )
    shared = jnp.concatenate([shared[:cut], jnp.sum(router_cut, axis=0)], axis=0)
    shared = a2a(jnp.broadcast_to(shared[None], (n_dp,) + shared.shape), "dp", 0)
    all_first = after(shared)
    grad_projection = shared[:, :cut].reshape(projection.shape)
    grad_router = shared[:, cut:].reshape(n_dp, cut_router * embed_width)[:, :width].T

    (grad_in,) = call(
        weight_kernel,
        [(hidden_dev, width)],
        (where, both, *blocks),
        us=10,
        mib=58,
        fetch=True,
    )
    grad_expert_in = grad_in.T
    transfer_img = mm_tn(sums[:pairs], grad_img)
    transfer_txt = mm_tn(sums[pairs:], grad_txt)
    grad_expert_out = mm_nt(transfer_img, projection_img) + mm_nt(transfer_txt, projection_txt)

    farthest = grads[4]
    ahead, behind = lax.optimization_barrier((step(farthest[half:], 1), step(farthest[:half], -1)))
    ahead, behind = lax.optimization_barrier(
        (
            step(jnp.concatenate([grads[3][:half], grads[3][half:] + ahead], axis=0), 1),
            step(jnp.concatenate([grads[5][:half] + behind, grads[5][half:]], axis=0), -1),
        )
    )
    ahead, behind = lax.optimization_barrier(
        (step(grads[2] + ahead, 1), step(grads[6] + behind, -1))
    )
    ahead, behind = lax.optimization_barrier(
        (
            step(grads[1] + ahead + shared_first, 1),
            step(grads[7] + behind + shared_first, -1),
        )
    )
    grad_rows = grads[0] + ahead + behind + all_first
    grad_back = a2a(grad_rows.reshape(CAP, n_dp, width), "dp", 1).reshape(CAP * experts, width)
    grad_dispatch = mm(onehot, grad_back, highest)

    own_img = lax.dynamic_slice_in_dim(grad_img, own_pair, 1, 0)
    own_txt = lax.dynamic_slice_in_dim(grad_txt, own_pair, 1, 0)
    grad_pooled = jnp.concatenate(
        [mm_nt(own_img, projection_img), mm_nt(own_txt, projection_txt)], axis=0
    )
    grad_output = mm_tn(modal_mask, grad_pooled / group_sizes[:, None], highest)
    grad_tokens = grad_output + mm_nt(grad_logits, router_weight, highest) + grad_dispatch
    losses = jnp.stack([contrast, entropy_terms[0], entropy_terms[1]])
    return (
        losses,
        grad_tokens,
        grad_router,
        grad_expert_in[None],
        grad_expert_out[None],
        grad_projection,
    )


def solution(mesh):
    return jax.shard_map(
        body,
        mesh=mesh,
        in_specs=(
            P(("dp", "expert"), None),
            P(),
            P("dp", None, "expert"),
            P("dp", "expert", None),
            P(None, "expert", None),
            P(("dp", "expert")),
            P(("dp", "expert")),
        ),
        out_specs=(
            P(),
            P(("dp", "expert"), None),
            P(),
            P("dp", None, "expert"),
            P("dp", "expert", None),
            P(None, "expert", None),
        ),
        check_vma=False,
    )
```

```python
import functools
import math

import jax
import jax.numpy as jnp
from jax import lax
from jax.experimental import pallas as pl
from jax.experimental.pallas import tpu as pltpu
from jax.sharding import PartitionSpec as P

highest = lax.Precision.HIGHEST
high = lax.Precision.HIGH
contrast_scale = 10.0
entropy_weight = 0.5
norm_epsilon = 1e-06
CAP = 5
PAIR_LEN = 128


def gelu_exact(values):
    return jax.nn.gelu(values, approximate=False)


def dot(a, b, dims, precision=high):
    return lax.dot_general(a, b, (dims, ((), ())), precision=precision)


def mm(a, b, precision=high):
    return dot(a, b, ((1,), (0,)), precision)


def mm_nt(a, b, precision=high):
    return dot(a, b, ((1,), (1,)), precision)


def mm_tn(a, b, precision=high):
    return dot(a, b, ((0,), (0,)), precision)


def a2a(values, axis_name, axis):
    return lax.all_to_all(values, axis_name, split_axis=axis, concat_axis=axis, tiled=True)


def gather(values, axis_name):
    return lax.all_gather(values, axis_name, axis=0, tiled=True)


def after(values):
    return jnp.minimum(jnp.abs(values[(0,) * values.ndim]), 0.0)


def halves(values):
    large = values.astype(jnp.bfloat16)
    return large, (values - large.astype(jnp.float32)).astype(jnp.bfloat16)


def weight_halves(values):
    large = lax.reduce_precision(values, exponent_bits=8, mantissa_bits=7)
    return large.astype(jnp.bfloat16), (values - large).astype(jnp.bfloat16)


def dot3(a, b, dims):
    def one(x, y):
        return lax.dot_general(x, y, (dims, ((), ())), preferred_element_type=jnp.float32)

    return one(a[0], b[0]) + (one(a[0], b[1]) + one(a[1], b[0]))


def call(kernel, shapes, args, us, mib=16, fetch=False):
    def whole(shape):
        if fetch:
            return pl.BlockSpec(shape, lambda i: (0,) * len(shape))
        return pl.BlockSpec(memory_space=pltpu.VMEM)

    return pl.pallas_call(
        kernel,
        out_shape=[jax.ShapeDtypeStruct(shape, jnp.float32) for shape in shapes],
        grid=(1,) if fetch else (),
        in_specs=[pl.BlockSpec(memory_space=pltpu.SMEM)] + [whole(a.shape) for a in args[1:]],
        out_specs=[whole(shape) for shape in shapes],
        compiler_params=pltpu.CompilerParams(vmem_limit_bytes=mib << 20),
        cost_estimate=pl.CostEstimate(
            flops=int(us * 1.1e9), bytes_accessed=1 << 20, transcendentals=0
        ),
    )(*args)


LANES = 128
NN = ((1,), (0,))
NT = ((1,), (1,))
TN = ((0,), (0,))


def forward_kernel(experts, where, rows, w_large, w_small, gated, slope):
    both = dot3(halves(rows[...]), (w_large[...], w_small[...]), NT)
    lane = lax.broadcasted_iota(jnp.int32, (both.shape[0], LANES), 1)
    exponent = jnp.where(lane < experts, jnp.exp(both[:, :LANES]), 0.0)
    probs = exponent / jnp.sum(exponent, axis=1, keepdims=True)
    slope[:, :LANES] = probs
    gate = jnp.sum(jnp.where(lane == where[1], probs, 0.0), axis=1, keepdims=True)
    pre = both[:, LANES:]
    normal = 0.5 * (1.0 + lax.erf(pre * math.sqrt(0.5)))
    gated[...] = gate * (pre * normal)
    density = jnp.exp(-0.5 * pre * pre) * (1.0 / math.sqrt(2.0 * math.pi))
    slope[:, LANES:] = gate * (normal + pre * density)


def slot_weights(meta, slot):
    in_image = slot < meta[:, 0:1]
    images = meta[:, 1:2]
    return (
        jnp.where(in_image, 1.0 / images, 0.0),
        jnp.where(in_image, 0.0, 1.0 / (PAIR_LEN - images)),
    )


def embed_kernel(n_z, n_dp, where, *refs):
    gated = refs[:n_z]
    meta, m_large, m_small, part, sums = refs[n_z:]
    for r in range(n_z):
        plane = (where[0] + r) & (n_z - 1)
        block = meta[plane]
        image = text = 0.0
        for slot in range(CAP):
            weight_img, weight_txt = slot_weights(block, float(slot))
            rows = gated[r][slot * n_dp : (slot + 1) * n_dp, :]
            image = image + weight_img * rows
            text = text + weight_txt * rows
        sums[0, :, pl.ds(plane, 1), :] = image[:, None]
        sums[1, :, pl.ds(plane, 1), :] = text[:, None]
    for m in range(2):
        rows = sums[m].reshape(n_dp * n_z, sums.shape[3])
        embed = dot3(halves(rows), (m_large[m], m_small[m]), NN)
        part[:, m * n_z : (m + 1) * n_z, :] = embed.reshape(n_dp, n_z, embed.shape[1])


def head_kernel(n_z, factor, where, every, m_large, m_small, grads, back, contrast):
    pairs = every.shape[0] * n_z
    width = every.shape[2]

    def unit_of(m):
        values = every[:, m * n_z : (m + 1) * n_z, :].reshape(pairs, width)
        radius = jnp.sqrt(jnp.sum(values * values, axis=1, keepdims=True) + norm_epsilon)
        return values / radius, radius

    def product(a, b, dims):
        return lax.dot_general(a, b, (dims, ((), ())), precision=highest)

    unit_img, radius_img = unit_of(0)
    unit_txt, radius_txt = unit_of(1)
    scores = contrast_scale * product(unit_img, unit_txt, NT)
    exp_scores = jnp.exp(scores)
    total_img = jnp.sum(exp_scores, axis=1, keepdims=True)
    total_txt = jnp.sum(exp_scores, axis=0, keepdims=True)
    shape = (pairs, pairs)
    same = lax.broadcasted_iota(jnp.int32, shape, 0) == lax.broadcasted_iota(jnp.int32, shape, 1)
    logs = (
        jnp.sum(jnp.log(total_img), axis=0, keepdims=True)
        + jnp.sum(jnp.log(total_txt), axis=1, keepdims=True)
    )
    matched = jnp.sum(jnp.where(same, scores, 0.0), axis=1, keepdims=True)
    matched = jnp.sum(matched, axis=0, keepdims=True)
    contrast[...] = jnp.broadcast_to((logs - 2.0 * matched) / (2.0 * pairs), contrast.shape)
    coupling = (
        exp_scores / total_img + exp_scores / total_txt - jnp.where(same, 2.0, 0.0)
    ) * factor
    for m, unit, radius, grad_unit in (
        (0, unit_img, radius_img, product(coupling, unit_txt, NN)),
        (1, unit_txt, radius_txt, product(coupling.T, unit_img, NN)),
    ):
        along = jnp.sum(unit * grad_unit, axis=1, keepdims=True)
        grad = (grad_unit - unit * along) / radius
        grads[m] = grad
        q = dot3(halves(grad), (m_large[m], m_small[m]), NT)
        back[m] = q.reshape(every.shape[0], n_z, q.shape[1])


def backward_kernel(n_z, n_dp, where, *refs):
    gated, slope = refs[:n_z], refs[n_z : 2 * n_z]
    meta, back, both = refs[2 * n_z :]
    lane = lax.broadcasted_iota(jnp.int32, (n_dp, LANES), 1)
    chosen = jnp.where(lane == where[1], 1.0, 0.0)
    slots = CAP * n_dp
    for r in range(n_z):
        plane = (where[0] + r) & (n_z - 1)
        back_img = back[0, :, pl.ds(plane, 1), :].reshape(n_dp, back.shape[3])
        back_txt = back[1, :, pl.ds(plane, 1), :].reshape(n_dp, back.shape[3])
        block = meta[plane]
        for slot in range(CAP):
            part = slice(slot * n_dp, (slot + 1) * n_dp)
            out = slice(r * slots + slot * n_dp, r * slots + (slot + 1) * n_dp)
            weight_img, weight_txt = slot_weights(block, float(slot))
            mixed = weight_img * back_img + weight_txt * back_txt
            both[out, LANES:] = slope[r][part, LANES:] * mixed
            log_gate = jnp.sum(gated[r][part, :] * mixed, axis=1, keepdims=True)
            both[out, :LANES] = log_gate * (chosen - slope[r][part, :LANES])


def router_kernel(where, both, *refs):
    blocks, out = refs[:-1], refs[-1]
    slots = blocks[0].shape[0]
    total = 0.0
    for r, rows in enumerate(blocks):
        logits = both[r * slots : (r + 1) * slots, :LANES]
        total = total + dot3(halves(logits), halves(rows[...]), TN)
    out[...] = total


def rows_kernel(which, where, both, w_large, w_small, *grad_rows):
    slots = grad_rows[0].shape[0]
    for r, out in zip(which, grad_rows):
        values = halves(both[r * slots : (r + 1) * slots, :])
        out[...] = dot3(values, (w_large[...], w_small[...]), NN)


def weight_kernel(where, both, *refs):
    blocks, out = refs[:-1], refs[-1]
    slots = blocks[0].shape[0]
    for r, rows in enumerate(blocks):
        values = halves(both[r * slots : (r + 1) * slots, LANES:])
        term = dot3(values, halves(rows[...]), TN)
        if r == 0:
            out[...] = term
        else:
            out[...] += term


def body(tokens, router_weight, expert_in, expert_out, projection, assignment, modality):
    tok_count, width = tokens.shape
    experts = router_weight.shape[1]
    n_dp = lax.axis_size("dp")
    n_z = lax.axis_size("expert")
    pairs = n_dp * n_z
    total_tokens = tok_count * pairs
    w_in = expert_in[0]
    w_out = expert_out[0]
    hidden_dev = w_in.shape[1]
    embed_width = projection.shape[2]
    my_dp = lax.axis_index("dp")
    my_z = lax.axis_index("expert")
    own_pair = my_dp * n_z + my_z
    where = jnp.stack([my_z, my_dp])
    my_core = my_dp & 1

    def step(values, shift):
        return lax.ppermute(values, "expert", [(i, (i + shift) % n_z) for i in range(n_z)])

    projection_mine = gather(jnp.where(my_core == 0, projection[0], projection[1]), "expert")
    projection_other = lax.ppermute(projection_mine, "dp", [(i, i ^ 1) for i in range(n_dp)])

    expert_ids = lax.broadcasted_iota(jnp.int32, (1, experts), 1)
    chosen_mask = (assignment[:, None] == expert_ids).astype(jnp.float32)
    before = (
        lax.broadcasted_iota(jnp.int32, (tok_count, tok_count), 0)
        > lax.broadcasted_iota(jnp.int32, (tok_count, tok_count), 1)
    ).astype(jnp.bfloat16)
    earlier = jnp.dot(
        before, chosen_mask.astype(jnp.bfloat16), preferred_element_type=jnp.float32
    )
    slot = jnp.sum(earlier * chosen_mask, axis=1).astype(jnp.int32)
    cell_ids = lax.broadcasted_iota(jnp.int32, (1, CAP * experts), 1)
    onehot = ((slot * experts + assignment)[:, None] == cell_ids).astype(jnp.float32)
    dispatched = mm_tn(onehot, tokens, highest).reshape(CAP, experts, width)
    received = a2a(dispatched, "dp", 1).reshape(CAP * n_dp, width)

    projection_img = jnp.where(my_core == 0, projection_mine, projection_other)
    projection_txt = jnp.where(my_core == 0, projection_other, projection_mine)
    mixed_img = mm(w_out, projection_img)
    mixed_txt = mm(w_out, projection_txt)
    mixed_first = after(projection_other)
    half = received.shape[0] // 2
    logits = mm(tokens, router_weight, highest)
    exponent = jnp.exp(logits)
    router_prob = exponent / jnp.sum(exponent, axis=1, keepdims=True)
    is_image = (modality == 0).astype(jnp.float32)
    modal_mask = jnp.stack([is_image, 1.0 - is_image], axis=0)
    images = jnp.sum(is_image)
    group_sizes = jnp.stack([images, tok_count - images])
    usage_part = mm(modal_mask, router_prob, highest).reshape(1, 2 * experts)
    image_slots = dot(chosen_mask, is_image, ((0,), (0,)), highest)
    meta = jnp.concatenate(
        [
            image_slots[:, None],
            jnp.broadcast_to(images, (experts, 1)),
            jnp.broadcast_to(usage_part, (experts, 2 * experts)),
            received[:experts, : 126 - 2 * experts],
        ],
        axis=1,
    )
    meta = a2a(meta, "dp", 0)
    meta_first = after(meta)
    meta = a2a(jnp.broadcast_to(meta[None], (n_z, n_dp, 128)), "expert", 0)
    left1, right1 = lax.optimization_barrier((step(received, -1), step(received, 1)))
    left2, right2 = lax.optimization_barrier((step(left1, -1), step(right1 + meta_first, 1)))
    left3, right3 = lax.optimization_barrier((step(left2, -1), step(right2, 1)))
    middle = jnp.concatenate(
        [step(left3[:half] + mixed_first, -1), step(right3[half:] + mixed_first, 1)], axis=0
    )
    blocks = [received, left1, left2, left3, middle, right3, right2, right1]

    token_means = mm(modal_mask / group_sizes[:, None], tokens, highest)

    embed_means = jnp.concatenate(
        [mm(token_means[:1], projection_img), mm(token_means[1:], projection_txt)], axis=0
    )

    usage_all = jnp.sum(meta[:, :, 2 : 2 + 2 * experts], axis=(0, 1)).reshape(2, experts)
    image_total = jnp.sum(meta[:, :, 1])
    count_sum = jnp.stack([image_total, total_tokens - image_total])

    slots = CAP * n_dp
    w_pair = weight_halves(
        jnp.concatenate(
            [jnp.pad(router_weight.T, ((0, LANES - experts), (0, 0))), w_in.T], axis=0
        )
    )
    wide = LANES + hidden_dev
    done = [
        call(
            functools.partial(forward_kernel, experts),
            [(slots, hidden_dev), (slots, wide)],
            (where, blocks[r], *w_pair),
            us=2.5,
        )
        for r in range(n_z)
    ]

    mixed_pair = weight_halves(jnp.stack([mixed_img, mixed_txt]))
    part, sums = call(
        functools.partial(embed_kernel, n_z, n_dp),
        [(n_dp, 2 * n_z, embed_width), (2, n_dp, n_z, hidden_dev)],
        (where, *[d[0] for d in done], meta, *mixed_pair),
        us=3,
        mib=58,
        fetch=True,
    )
    sums = sums.reshape(2 * pairs, hidden_dev)
    column_ids = lax.broadcasted_iota(jnp.int32, (1, 2 * pairs), 1)
    pooled_part = (
        dot(w_out, sums, ((0,), (1,)))
        + jnp.where(column_ids == own_pair, token_means[0][:, None], 0.0)
        + jnp.where(column_ids == own_pair + pairs, token_means[1][:, None], 0.0)
    )
    pooled_cut = lax.psum_scatter(pooled_part, "expert", scatter_dimension=0, tiled=True)
    pooled_first = after(pooled_part)
    part = jnp.sum(a2a(part, "dp", 0), axis=0).reshape(2, n_z, embed_width)
    own_plane = lax.broadcasted_iota(jnp.int32, (1, n_z, 1), 1) == my_z
    part = part + jnp.where(own_plane, embed_means[:, None], 0.0) + pooled_first
    part = a2a(jnp.broadcast_to(part[None], (n_z, 2, n_z, embed_width)), "expert", 0)
    column = jnp.sum(part, axis=0).reshape(1, 2 * n_z, embed_width)
    every = a2a(jnp.broadcast_to(column, (n_dp, 2 * n_z, embed_width)), "dp", 0)
    pair_grads, back, contrast = call(
        functools.partial(
            head_kernel, n_z, contrast_scale * total_tokens / (2.0 * pairs)
        ),
        [(2, pairs, embed_width), (2, n_dp, n_z, hidden_dev), (8, LANES)],
        (where, every, *mixed_pair),
        us=5,
        mib=58,
        fetch=True,
    )
    grad_img, grad_txt = pair_grads[0], pair_grads[1]
    contrast = contrast[0, 0]

    (both,) = call(
        functools.partial(backward_kernel, n_z, n_dp),
        [(n_z * slots, wide)],
        (where, *[d[0] for d in done], *[d[1] for d in done], meta, back),
        us=4,
        mib=58,
        fetch=True,
    )
    grads = {}
    for which in ((4,), (3, 5), (2, 6), (1, 7, 0)):
        made = call(
            functools.partial(rows_kernel, which),
            [(slots, width)] * len(which),
            (where, both, *w_pair),
            us=1.8 * len(which),
        )
        grads.update(zip(which, made))

    mean_usage = usage_all / count_sum[:, None]
    log_usage = jnp.log(mean_usage)
    entropy_terms = jnp.sum(mean_usage * log_usage, axis=1)
    usage_factor = entropy_weight * total_tokens * (log_usage + 1.0) / count_sum[:, None]
    grad_prob = mm_tn(modal_mask, usage_factor, highest)
    grad_logits = router_prob * (
        grad_prob - jnp.sum(router_prob * grad_prob, axis=1, keepdims=True)
    )

    pooled_done = after(pooled_cut)
    projection_part = jnp.concatenate(
        [mm(pooled_cut[:, :pairs], grad_img), mm(pooled_cut[:, pairs:], grad_txt)], axis=0
    )
    cut = projection_part.shape[0] // n_dp
    (router_sum,) = call(
        router_kernel,
        [(LANES, width)],
        (where, both, *blocks),
        us=6,
        mib=58,
        fetch=True,
    )
    router_part = router_sum[:experts] + mm_tn(grad_logits, tokens)
    cut_router = -(-width // embed_width)
    router_part = jnp.pad(router_part, ((0, 0), (0, cut_router * embed_width - width)))
    shared = jnp.concatenate(
        [
            projection_part.reshape(n_dp, cut, embed_width),
            router_part.reshape(n_dp, cut_router, embed_width),
        ],
        axis=1,
    )
    made_first = after(shared)
    shared = jnp.sum(a2a(shared, "dp", 0), axis=0)
    shared_first = after(shared)
    router_cut = a2a(
        jnp.broadcast_to(shared[None, cut:], (n_z, cut_router, embed_width)), "expert", 0
    )
    shared = jnp.concatenate([shared[:cut], jnp.sum(router_cut, axis=0)], axis=0)
    shared = a2a(jnp.broadcast_to(shared[None], (n_dp,) + shared.shape), "dp", 0)
    all_first = after(shared)
    grad_projection = shared[:, :cut].reshape(projection.shape)
    grad_router = shared[:, cut:].reshape(n_dp, cut_router * embed_width)[:, :width].T

    (grad_in,) = call(
        weight_kernel,
        [(hidden_dev, width)],
        (where, both, *blocks),
        us=10,
        mib=58,
        fetch=True,
    )
    grad_expert_in = grad_in.T
    transfer_img = mm_tn(sums[:pairs], grad_img)
    transfer_txt = mm_tn(sums[pairs:], grad_txt)
    grad_expert_out = mm_nt(transfer_img, projection_img) + mm_nt(transfer_txt, projection_txt)

    farthest = grads[4]
    ahead, behind = lax.optimization_barrier((step(farthest[half:], 1), step(farthest[:half], -1)))
    ahead, behind = lax.optimization_barrier(
        (
            step(jnp.concatenate([grads[3][:half], grads[3][half:] + (ahead + pooled_done)], axis=0), 1),
            step(jnp.concatenate([grads[5][:half] + (behind + pooled_done), grads[5][half:]], axis=0), -1),
        )
    )
    ahead, behind = lax.optimization_barrier(
        (step(grads[2] + ahead + made_first, 1), step(grads[6] + behind + made_first, -1))
    )
    ahead, behind = lax.optimization_barrier(
        (
            step(grads[1] + ahead + shared_first, 1),
            step(grads[7] + behind + shared_first, -1),
        )
    )
    grad_rows = grads[0] + ahead + behind + all_first
    grad_back = a2a(grad_rows.reshape(CAP, n_dp, width), "dp", 1).reshape(CAP * experts, width)
    grad_dispatch = mm(onehot, grad_back, highest)

    own_img = lax.dynamic_slice_in_dim(grad_img, own_pair, 1, 0)
    own_txt = lax.dynamic_slice_in_dim(grad_txt, own_pair, 1, 0)
    grad_pooled = jnp.concatenate(
        [mm_nt(own_img, projection_img), mm_nt(own_txt, projection_txt)], axis=0
    )
    grad_output = mm_tn(modal_mask, grad_pooled / group_sizes[:, None], highest)
    grad_tokens = grad_output + mm_nt(grad_logits, router_weight, highest) + grad_dispatch
    losses = jnp.stack([contrast, entropy_terms[0], entropy_terms[1]])
    return (
        losses,
        grad_tokens,
        grad_router,
        grad_expert_in[None],
        grad_expert_out[None],
        grad_projection,
    )


def solution(mesh):
    return jax.shard_map(
        body,
        mesh=mesh,
        in_specs=(
            P(("dp", "expert"), None),
            P(),
            P("dp", None, "expert"),
            P("dp", "expert", None),
            P(None, "expert", None),
            P(("dp", "expert")),
            P(("dp", "expert")),
        ),
        out_specs=(
            P(),
            P(("dp", "expert"), None),
            P(),
            P("dp", None, "expert"),
            P("dp", "expert", None),
            P(None, "expert", None),
        ),
        check_vma=False,
    )
```

```python
import functools
import math

import jax
import jax.numpy as jnp
from jax import lax
from jax.experimental import pallas as pl
from jax.experimental.pallas import tpu as pltpu
from jax.sharding import PartitionSpec as P

highest = lax.Precision.HIGHEST
high = lax.Precision.HIGH
contrast_scale = 10.0
entropy_weight = 0.5
norm_epsilon = 1e-06
CAP = 5
PAIR_LEN = 128


def gelu_exact(values):
    return jax.nn.gelu(values, approximate=False)


def dot(a, b, dims, precision=high):
    return lax.dot_general(a, b, (dims, ((), ())), precision=precision)


def mm(a, b, precision=high):
    return dot(a, b, ((1,), (0,)), precision)


def mm_nt(a, b, precision=high):
    return dot(a, b, ((1,), (1,)), precision)


def mm_tn(a, b, precision=high):
    return dot(a, b, ((0,), (0,)), precision)


def a2a(values, axis_name, axis):
    return lax.all_to_all(values, axis_name, split_axis=axis, concat_axis=axis, tiled=True)


def gather(values, axis_name):
    return lax.all_gather(values, axis_name, axis=0, tiled=True)


def after(values):
    return jnp.minimum(jnp.abs(values[(0,) * values.ndim]), 0.0)


def halves(values):
    large = values.astype(jnp.bfloat16)
    return large, (values - large.astype(jnp.float32)).astype(jnp.bfloat16)


def weight_halves(values):
    large = lax.reduce_precision(values, exponent_bits=8, mantissa_bits=7)
    return large.astype(jnp.bfloat16), (values - large).astype(jnp.bfloat16)


def dot3(a, b, dims):
    def one(x, y):
        return lax.dot_general(x, y, (dims, ((), ())), preferred_element_type=jnp.float32)

    return one(a[0], b[0]) + (one(a[0], b[1]) + one(a[1], b[0]))


def call(kernel, shapes, args, us, mib=16, fetch=False):
    def whole(shape):
        if fetch:
            return pl.BlockSpec(shape, lambda i: (0,) * len(shape))
        return pl.BlockSpec(memory_space=pltpu.VMEM)

    return pl.pallas_call(
        kernel,
        out_shape=[jax.ShapeDtypeStruct(shape, jnp.float32) for shape in shapes],
        grid=(1,) if fetch else (),
        in_specs=[pl.BlockSpec(memory_space=pltpu.SMEM)] + [whole(a.shape) for a in args[1:]],
        out_specs=[whole(shape) for shape in shapes],
        compiler_params=pltpu.CompilerParams(vmem_limit_bytes=mib << 20),
        cost_estimate=pl.CostEstimate(
            flops=int(us * 1.1e9), bytes_accessed=1 << 20, transcendentals=0
        ),
    )(*args)


LANES = 128
NN = ((1,), (0,))
NT = ((1,), (1,))
TN = ((0,), (0,))


def forward_kernel(experts, where, rows, w_large, w_small, gated, slope):
    both = dot3(halves(rows[...]), (w_large[...], w_small[...]), NT)
    lane = lax.broadcasted_iota(jnp.int32, (both.shape[0], LANES), 1)
    exponent = jnp.where(lane < experts, jnp.exp(both[:, :LANES]), 0.0)
    probs = exponent / jnp.sum(exponent, axis=1, keepdims=True)
    slope[:, :LANES] = probs
    gate = jnp.sum(jnp.where(lane == where[1], probs, 0.0), axis=1, keepdims=True)
    pre = both[:, LANES:]
    normal = 0.5 * (1.0 + lax.erf(pre * math.sqrt(0.5)))
    gated[...] = gate * (pre * normal)
    density = jnp.exp(-0.5 * pre * pre) * (1.0 / math.sqrt(2.0 * math.pi))
    slope[:, LANES:] = gate * (normal + pre * density)


def slot_weights(meta, slot):
    in_image = slot < meta[:, 0:1]
    images = meta[:, 1:2]
    return (
        jnp.where(in_image, 1.0 / images, 0.0),
        jnp.where(in_image, 0.0, 1.0 / (PAIR_LEN - images)),
    )


def embed_kernel(n_z, n_dp, where, *refs):
    gated = refs[:n_z]
    meta, m_large, m_small, part, sums = refs[n_z:]
    for r in range(n_z):
        plane = (where[0] + r) & (n_z - 1)
        block = meta[plane]
        image = text = 0.0
        for slot in range(CAP):
            weight_img, weight_txt = slot_weights(block, float(slot))
            rows = gated[r][slot * n_dp : (slot + 1) * n_dp, :]
            image = image + weight_img * rows
            text = text + weight_txt * rows
        sums[0, :, pl.ds(plane, 1), :] = image[:, None]
        sums[1, :, pl.ds(plane, 1), :] = text[:, None]
    for m in range(2):
        rows = sums[m].reshape(n_dp * n_z, sums.shape[3])
        embed = dot3(halves(rows), (m_large[m], m_small[m]), NN)
        part[:, m * n_z : (m + 1) * n_z, :] = embed.reshape(n_dp, n_z, embed.shape[1])


def head_kernel(n_z, factor, where, every, m_large, m_small, grads, back, contrast):
    pairs = every.shape[0] * n_z
    width = every.shape[2]

    def unit_of(m):
        values = every[:, m * n_z : (m + 1) * n_z, :].reshape(pairs, width)
        radius = jnp.sqrt(jnp.sum(values * values, axis=1, keepdims=True) + norm_epsilon)
        return values / radius, radius

    def product(a, b, dims):
        return lax.dot_general(a, b, (dims, ((), ())), precision=highest)

    unit_img, radius_img = unit_of(0)
    unit_txt, radius_txt = unit_of(1)
    scores = contrast_scale * product(unit_img, unit_txt, NT)
    exp_scores = jnp.exp(scores)
    total_img = jnp.sum(exp_scores, axis=1, keepdims=True)
    total_txt = jnp.sum(exp_scores, axis=0, keepdims=True)
    shape = (pairs, pairs)
    same = lax.broadcasted_iota(jnp.int32, shape, 0) == lax.broadcasted_iota(jnp.int32, shape, 1)
    logs = (
        jnp.sum(jnp.log(total_img), axis=0, keepdims=True)
        + jnp.sum(jnp.log(total_txt), axis=1, keepdims=True)
    )
    matched = jnp.sum(jnp.where(same, scores, 0.0), axis=1, keepdims=True)
    matched = jnp.sum(matched, axis=0, keepdims=True)
    contrast[...] = jnp.broadcast_to((logs - 2.0 * matched) / (2.0 * pairs), contrast.shape)
    coupling = (
        exp_scores / total_img + exp_scores / total_txt - jnp.where(same, 2.0, 0.0)
    ) * factor
    for m, unit, radius, grad_unit in (
        (0, unit_img, radius_img, product(coupling, unit_txt, NN)),
        (1, unit_txt, radius_txt, product(coupling.T, unit_img, NN)),
    ):
        along = jnp.sum(unit * grad_unit, axis=1, keepdims=True)
        grad = (grad_unit - unit * along) / radius
        grads[m] = grad
        q = dot3(halves(grad), (m_large[m], m_small[m]), NT)
        back[m] = q.reshape(every.shape[0], n_z, q.shape[1])


def backward_kernel(n_z, n_dp, where, *refs):
    gated, slope = refs[:n_z], refs[n_z : 2 * n_z]
    meta, back, both = refs[2 * n_z :]
    lane = lax.broadcasted_iota(jnp.int32, (n_dp, LANES), 1)
    chosen = jnp.where(lane == where[1], 1.0, 0.0)
    slots = CAP * n_dp
    for r in range(n_z):
        plane = (where[0] + r) & (n_z - 1)
        back_img = back[0, :, pl.ds(plane, 1), :].reshape(n_dp, back.shape[3])
        back_txt = back[1, :, pl.ds(plane, 1), :].reshape(n_dp, back.shape[3])
        block = meta[plane]
        for slot in range(CAP):
            part = slice(slot * n_dp, (slot + 1) * n_dp)
            out = slice(r * slots + slot * n_dp, r * slots + (slot + 1) * n_dp)
            weight_img, weight_txt = slot_weights(block, float(slot))
            mixed = weight_img * back_img + weight_txt * back_txt
            both[out, LANES:] = slope[r][part, LANES:] * mixed
            log_gate = jnp.sum(gated[r][part, :] * mixed, axis=1, keepdims=True)
            both[out, :LANES] = log_gate * (chosen - slope[r][part, :LANES])


def router_kernel(where, both, *refs):
    blocks, out = refs[:-1], refs[-1]
    slots = blocks[0].shape[0]
    total = 0.0
    for r, rows in enumerate(blocks):
        logits = both[r * slots : (r + 1) * slots, :LANES]
        total = total + dot3(halves(logits), halves(rows[...]), TN)
    out[...] = total


def rows_kernel(which, where, both, w_large, w_small, *grad_rows):
    slots = grad_rows[0].shape[0]
    for r, out in zip(which, grad_rows):
        values = halves(both[r * slots : (r + 1) * slots, :])
        out[...] = dot3(values, (w_large[...], w_small[...]), NN)


def weight_kernel(where, both, *refs):
    blocks, out = refs[:-1], refs[-1]
    slots = blocks[0].shape[0]
    for r, rows in enumerate(blocks):
        values = halves(both[r * slots : (r + 1) * slots, LANES:])
        term = dot3(values, halves(rows[...]), TN)
        if r == 0:
            out[...] = term
        else:
            out[...] += term


def body(tokens, router_weight, expert_in, expert_out, projection, assignment, modality):
    tok_count, width = tokens.shape
    experts = router_weight.shape[1]
    n_dp = lax.axis_size("dp")
    n_z = lax.axis_size("expert")
    pairs = n_dp * n_z
    total_tokens = tok_count * pairs
    w_in = expert_in[0]
    w_out = expert_out[0]
    hidden_dev = w_in.shape[1]
    embed_width = projection.shape[2]
    my_dp = lax.axis_index("dp")
    my_z = lax.axis_index("expert")
    own_pair = my_dp * n_z + my_z
    where = jnp.stack([my_z, my_dp])
    my_core = my_dp & 1

    def step(values, shift):
        return lax.ppermute(values, "expert", [(i, (i + shift) % n_z) for i in range(n_z)])

    projection_mine = gather(jnp.where(my_core == 0, projection[0], projection[1]), "expert")
    projection_other = lax.ppermute(projection_mine, "dp", [(i, i ^ 1) for i in range(n_dp)])

    expert_ids = lax.broadcasted_iota(jnp.int32, (1, experts), 1)
    chosen_mask = (assignment[:, None] == expert_ids).astype(jnp.float32)
    before = (
        lax.broadcasted_iota(jnp.int32, (tok_count, tok_count), 0)
        > lax.broadcasted_iota(jnp.int32, (tok_count, tok_count), 1)
    ).astype(jnp.bfloat16)
    earlier = jnp.dot(
        before, chosen_mask.astype(jnp.bfloat16), preferred_element_type=jnp.float32
    )
    slot = jnp.sum(earlier * chosen_mask, axis=1).astype(jnp.int32)
    cell_ids = lax.broadcasted_iota(jnp.int32, (1, CAP * experts), 1)
    onehot = ((slot * experts + assignment)[:, None] == cell_ids).astype(jnp.float32)
    dispatched = mm_tn(onehot, tokens, highest).reshape(CAP, experts, width)
    received = a2a(dispatched, "dp", 1).reshape(CAP * n_dp, width)

    projection_img = jnp.where(my_core == 0, projection_mine, projection_other)
    projection_txt = jnp.where(my_core == 0, projection_other, projection_mine)
    mixed_img = mm(w_out, projection_img)
    mixed_txt = mm(w_out, projection_txt)
    mixed_first = after(mixed_img) + after(mixed_txt)
    half = received.shape[0] // 2
    logits = mm(tokens, router_weight, highest)
    exponent = jnp.exp(logits)
    router_prob = exponent / jnp.sum(exponent, axis=1, keepdims=True)
    is_image = (modality == 0).astype(jnp.float32)
    modal_mask = jnp.stack([is_image, 1.0 - is_image], axis=0)
    images = jnp.sum(is_image)
    group_sizes = jnp.stack([images, tok_count - images])
    usage_part = mm(modal_mask, router_prob, highest).reshape(1, 2 * experts)
    image_slots = dot(chosen_mask, is_image, ((0,), (0,)), highest)
    meta = jnp.concatenate(
        [
            image_slots[:, None],
            jnp.broadcast_to(images, (experts, 1)),
            jnp.broadcast_to(usage_part, (experts, 2 * experts)),
            received[:experts, : 126 - 2 * experts],
        ],
        axis=1,
    )
    meta = a2a(meta, "dp", 0)
    meta_first = after(meta)
    meta = a2a(jnp.broadcast_to(meta[None], (n_z, n_dp, 128)), "expert", 0)
    left1, right1 = lax.optimization_barrier((step(received, -1), step(received, 1)))
    left2, right2 = lax.optimization_barrier((step(left1, -1), step(right1 + meta_first, 1)))
    left3, right3 = lax.optimization_barrier((step(left2, -1), step(right2, 1)))
    middle = jnp.concatenate(
        [step(left3[:half] + mixed_first, -1), step(right3[half:] + mixed_first, 1)], axis=0
    )
    blocks = [received, left1, left2, left3, middle, right3, right2, right1]

    token_means = mm(modal_mask / group_sizes[:, None], tokens, highest)

    embed_means = jnp.concatenate(
        [mm(token_means[:1], projection_img), mm(token_means[1:], projection_txt)], axis=0
    )

    usage_all = jnp.sum(meta[:, :, 2 : 2 + 2 * experts], axis=(0, 1)).reshape(2, experts)
    image_total = jnp.sum(meta[:, :, 1])
    count_sum = jnp.stack([image_total, total_tokens - image_total])

    slots = CAP * n_dp
    w_pair = weight_halves(
        jnp.concatenate(
            [jnp.pad(router_weight.T, ((0, LANES - experts), (0, 0))), w_in.T], axis=0
        )
    )
    wide = LANES + hidden_dev
    done = [
        call(
            functools.partial(forward_kernel, experts),
            [(slots, hidden_dev), (slots, wide)],
            (where, blocks[r], *w_pair),
            us=2.5,
        )
        for r in range(n_z)
    ]

    mixed_pair = weight_halves(jnp.stack([mixed_img, mixed_txt]))
    part, sums = call(
        functools.partial(embed_kernel, n_z, n_dp),
        [(n_dp, 2 * n_z, embed_width), (2, n_dp, n_z, hidden_dev)],
        (where, *[d[0] for d in done], meta, *mixed_pair),
        us=3,
        mib=58,
        fetch=True,
    )
    sums = sums.reshape(2 * pairs, hidden_dev)
    column_ids = lax.broadcasted_iota(jnp.int32, (1, 2 * pairs), 1)
    pooled_part = (
        dot(w_out, sums, ((0,), (1,)))
        + jnp.where(column_ids == own_pair, token_means[0][:, None], 0.0)
        + jnp.where(column_ids == own_pair + pairs, token_means[1][:, None], 0.0)
    )
    pooled_first = after(pooled_part)
    pooled_cut = lax.psum_scatter(pooled_part, "expert", scatter_dimension=0, tiled=True)
    head_where = where + after(pooled_cut).astype(jnp.int32)
    part = jnp.sum(a2a(part, "dp", 0), axis=0).reshape(2, n_z, embed_width)
    own_plane = lax.broadcasted_iota(jnp.int32, (1, n_z, 1), 1) == my_z
    part = part + jnp.where(own_plane, embed_means[:, None], 0.0) + pooled_first
    part = a2a(jnp.broadcast_to(part[None], (n_z, 2, n_z, embed_width)), "expert", 0)
    column = jnp.sum(part, axis=0).reshape(1, 2 * n_z, embed_width)
    every = a2a(jnp.broadcast_to(column, (n_dp, 2 * n_z, embed_width)), "dp", 0)
    pair_grads, back, contrast = call(
        functools.partial(
            head_kernel, n_z, contrast_scale * total_tokens / (2.0 * pairs)
        ),
        [(2, pairs, embed_width), (2, n_dp, n_z, hidden_dev), (8, LANES)],
        (head_where, every, *mixed_pair),
        us=5,
        mib=58,
        fetch=True,
    )
    grad_img, grad_txt = pair_grads[0], pair_grads[1]
    contrast = contrast[0, 0]

    (both,) = call(
        functools.partial(backward_kernel, n_z, n_dp),
        [(n_z * slots, wide)],
        (where, *[d[0] for d in done], *[d[1] for d in done], meta, back),
        us=4,
        mib=58,
        fetch=True,
    )
    grads = {}

    def rows_of(which, where):
        made = call(
            functools.partial(rows_kernel, which),
            [(slots, width)] * len(which),
            (where, both, *w_pair),
            us=1.8 * len(which),
        )
        grads.update(zip(which, made))

    rows_of((4,), where)
    farthest = grads[4]
    ahead, behind = lax.optimization_barrier((step(farthest[half:], 1), step(farthest[:half], -1)))
    sent = after(ahead)
    sent_where = where + sent.astype(jnp.int32)
    rows_of((3, 5), where)
    rows_of((2, 6), where)
    rows_of((1, 7, 0), sent_where)

    mean_usage = usage_all / count_sum[:, None]
    log_usage = jnp.log(mean_usage)
    entropy_terms = jnp.sum(mean_usage * log_usage, axis=1)
    usage_factor = entropy_weight * total_tokens * (log_usage + 1.0) / count_sum[:, None]
    grad_prob = mm_tn(modal_mask, usage_factor, highest)
    grad_logits = router_prob * (
        grad_prob - jnp.sum(router_prob * grad_prob, axis=1, keepdims=True)
    )

    projection_part = jnp.concatenate(
        [mm(pooled_cut[:, :pairs], grad_img), mm(pooled_cut[:, pairs:], grad_txt)], axis=0
    )
    cut = projection_part.shape[0] // n_dp
    (router_sum,) = call(
        router_kernel,
        [(LANES, width)],
        (sent_where, both, *blocks),
        us=6,
        mib=58,
        fetch=True,
    )
    router_part = router_sum[:experts] + mm_tn(grad_logits, tokens)
    cut_router = -(-width // embed_width)
    router_part = jnp.pad(router_part, ((0, 0), (0, cut_router * embed_width - width)))
    shared = jnp.concatenate(
        [
            projection_part.reshape(n_dp, cut, embed_width),
            router_part.reshape(n_dp, cut_router, embed_width),
        ],
        axis=1,
    )
    made_first = after(shared)
    shared = jnp.sum(a2a(shared, "dp", 0), axis=0)
    shared_first = after(shared)
    router_cut = a2a(
        jnp.broadcast_to(shared[None, cut:], (n_z, cut_router, embed_width)), "expert", 0
    )
    shared = jnp.concatenate([shared[:cut], jnp.sum(router_cut, axis=0)], axis=0)
    shared = a2a(jnp.broadcast_to(shared[None], (n_dp,) + shared.shape), "dp", 0)
    all_first = after(shared)
    grad_projection = shared[:, :cut].reshape(projection.shape)
    grad_router = shared[:, cut:].reshape(n_dp, cut_router * embed_width)[:, :width].T

    transfer_img = mm_tn(sums[:pairs], grad_img + sent)
    transfer_txt = mm_tn(sums[pairs:], grad_txt + sent)
    grad_expert_out = mm_nt(transfer_img, projection_img) + mm_nt(transfer_txt, projection_txt)

    ahead, behind = lax.optimization_barrier(
        (
            step(jnp.concatenate([grads[3][:half], grads[3][half:] + ahead], axis=0), 1),
            step(jnp.concatenate([grads[5][:half] + behind, grads[5][half:]], axis=0), -1),
        )
    )
    (grad_in,) = call(
        weight_kernel,
        [(hidden_dev, width)],
        (where + after(ahead).astype(jnp.int32), both, *blocks),
        us=10,
        mib=58,
        fetch=True,
    )
    grad_expert_in = grad_in.T
    ahead, behind = lax.optimization_barrier(
        (step(grads[2] + ahead + made_first, 1), step(grads[6] + behind + made_first, -1))
    )
    ahead, behind = lax.optimization_barrier(
        (
            step(grads[1] + ahead + shared_first, 1),
            step(grads[7] + behind + shared_first, -1),
        )
    )
    grad_rows = grads[0] + ahead + behind + all_first
    grad_back = a2a(grad_rows.reshape(CAP, n_dp, width), "dp", 1).reshape(CAP * experts, width)
    grad_dispatch = mm(onehot, grad_back, highest)

    own_img = lax.dynamic_slice_in_dim(grad_img, own_pair, 1, 0)
    own_txt = lax.dynamic_slice_in_dim(grad_txt, own_pair, 1, 0)
    grad_pooled = jnp.concatenate(
        [mm_nt(own_img + sent, projection_img), mm_nt(own_txt + sent, projection_txt)], axis=0
    )
    grad_output = mm_tn(modal_mask, grad_pooled / group_sizes[:, None], highest)
    grad_tokens = grad_output + mm_nt(grad_logits, router_weight, highest) + grad_dispatch
    losses = jnp.stack([contrast, entropy_terms[0], entropy_terms[1]])
    return (
        losses,
        grad_tokens,
        grad_router,
        grad_expert_in[None],
        grad_expert_out[None],
        grad_projection,
    )


def solution(mesh):
    return jax.shard_map(
        body,
        mesh=mesh,
        in_specs=(
            P(("dp", "expert"), None),
            P(),
            P("dp", None, "expert"),
            P("dp", "expert", None),
            P(None, "expert", None),
            P(("dp", "expert")),
            P(("dp", "expert")),
        ),
        out_specs=(
            P(),
            P(("dp", "expert"), None),
            P(),
            P("dp", None, "expert"),
            P("dp", "expert", None),
            P(None, "expert", None),
        ),
        check_vma=False,
    )
```

```python
import functools
import math

import jax
import jax.numpy as jnp
from jax import lax
from jax.experimental import pallas as pl
from jax.experimental.pallas import tpu as pltpu
from jax.sharding import PartitionSpec as P

highest = lax.Precision.HIGHEST
high = lax.Precision.HIGH
contrast_scale = 10.0
entropy_weight = 0.5
norm_epsilon = 1e-06
CAP = 5
PAIR_LEN = 128


def gelu_exact(values):
    return jax.nn.gelu(values, approximate=False)


def dot(a, b, dims, precision=high):
    return lax.dot_general(a, b, (dims, ((), ())), precision=precision)


def mm(a, b, precision=high):
    return dot(a, b, ((1,), (0,)), precision)


def mm_nt(a, b, precision=high):
    return dot(a, b, ((1,), (1,)), precision)


def mm_tn(a, b, precision=high):
    return dot(a, b, ((0,), (0,)), precision)


def a2a(values, axis_name, axis):
    return lax.all_to_all(values, axis_name, split_axis=axis, concat_axis=axis, tiled=True)


def gather(values, axis_name):
    return lax.all_gather(values, axis_name, axis=0, tiled=True)


def after(values):
    return jnp.minimum(jnp.abs(values[(0,) * values.ndim]), 0.0)


def halves(values):
    large = values.astype(jnp.bfloat16)
    return large, (values - large.astype(jnp.float32)).astype(jnp.bfloat16)


def weight_halves(values):
    large = lax.reduce_precision(values, exponent_bits=8, mantissa_bits=7)
    return large.astype(jnp.bfloat16), (values - large).astype(jnp.bfloat16)


def dot3(a, b, dims):
    def one(x, y):
        return lax.dot_general(x, y, (dims, ((), ())), preferred_element_type=jnp.float32)

    return one(a[0], b[0]) + (one(a[0], b[1]) + one(a[1], b[0]))


def call(kernel, shapes, args, us, mib=16, fetch=False):
    def whole(shape):
        if fetch:
            return pl.BlockSpec(shape, lambda i: (0,) * len(shape))
        return pl.BlockSpec(memory_space=pltpu.VMEM)

    return pl.pallas_call(
        kernel,
        out_shape=[jax.ShapeDtypeStruct(shape, jnp.float32) for shape in shapes],
        grid=(1,) if fetch else (),
        in_specs=[pl.BlockSpec(memory_space=pltpu.SMEM)] + [whole(a.shape) for a in args[1:]],
        out_specs=[whole(shape) for shape in shapes],
        compiler_params=pltpu.CompilerParams(vmem_limit_bytes=mib << 20),
        cost_estimate=pl.CostEstimate(
            flops=int(us * 1.1e9), bytes_accessed=1 << 20, transcendentals=0
        ),
    )(*args)


LANES = 128
NN = ((1,), (0,))
NT = ((1,), (1,))
TN = ((0,), (0,))


def forward_kernel(experts, where, rows, w_large, w_small, gated, slope):
    both = dot3(halves(rows[...]), (w_large[...], w_small[...]), NT)
    lane = lax.broadcasted_iota(jnp.int32, (both.shape[0], LANES), 1)
    exponent = jnp.where(lane < experts, jnp.exp(both[:, :LANES]), 0.0)
    probs = exponent / jnp.sum(exponent, axis=1, keepdims=True)
    slope[:, :LANES] = probs
    gate = jnp.sum(jnp.where(lane == where[1], probs, 0.0), axis=1, keepdims=True)
    pre = both[:, LANES:]
    normal = 0.5 * (1.0 + lax.erf(pre * math.sqrt(0.5)))
    gated[...] = gate * (pre * normal)
    density = jnp.exp(-0.5 * pre * pre) * (1.0 / math.sqrt(2.0 * math.pi))
    slope[:, LANES:] = gate * (normal + pre * density)


def slot_weights(meta, slot):
    in_image = slot < meta[:, 0:1]
    images = meta[:, 1:2]
    return (
        jnp.where(in_image, 1.0 / images, 0.0),
        jnp.where(in_image, 0.0, 1.0 / (PAIR_LEN - images)),
    )


def embed_kernel(n_z, n_dp, where, *refs):
    gated = refs[:n_z]
    meta, m_large, m_small, part, sums = refs[n_z:]
    for r in range(n_z):
        plane = (where[0] + r) & (n_z - 1)
        block = meta[plane]
        image = text = 0.0
        for slot in range(CAP):
            weight_img, weight_txt = slot_weights(block, float(slot))
            rows = gated[r][slot * n_dp : (slot + 1) * n_dp, :]
            image = image + weight_img * rows
            text = text + weight_txt * rows
        sums[0, :, pl.ds(plane, 1), :] = image[:, None]
        sums[1, :, pl.ds(plane, 1), :] = text[:, None]
    for m in range(2):
        rows = sums[m].reshape(n_dp * n_z, sums.shape[3])
        embed = dot3(halves(rows), (m_large[m], m_small[m]), NN)
        part[:, m * n_z : (m + 1) * n_z, :] = embed.reshape(n_dp, n_z, embed.shape[1])


def head_kernel(n_z, factor, where, every, m_large, m_small, grads, back, contrast):
    pairs = every.shape[0] * n_z
    width = every.shape[2]

    def unit_of(m):
        values = every[:, m * n_z : (m + 1) * n_z, :].reshape(pairs, width)
        radius = jnp.sqrt(jnp.sum(values * values, axis=1, keepdims=True) + norm_epsilon)
        return values / radius, radius

    def product(a, b, dims):
        return lax.dot_general(a, b, (dims, ((), ())), precision=highest)

    unit_img, radius_img = unit_of(0)
    unit_txt, radius_txt = unit_of(1)
    scores = contrast_scale * product(unit_img, unit_txt, NT)
    exp_scores = jnp.exp(scores)
    total_img = jnp.sum(exp_scores, axis=1, keepdims=True)
    total_txt = jnp.sum(exp_scores, axis=0, keepdims=True)
    shape = (pairs, pairs)
    same = lax.broadcasted_iota(jnp.int32, shape, 0) == lax.broadcasted_iota(jnp.int32, shape, 1)
    logs = (
        jnp.sum(jnp.log(total_img), axis=0, keepdims=True)
        + jnp.sum(jnp.log(total_txt), axis=1, keepdims=True)
    )
    matched = jnp.sum(jnp.where(same, scores, 0.0), axis=1, keepdims=True)
    matched = jnp.sum(matched, axis=0, keepdims=True)
    contrast[...] = jnp.broadcast_to((logs - 2.0 * matched) / (2.0 * pairs), contrast.shape)
    coupling = (
        exp_scores / total_img + exp_scores / total_txt - jnp.where(same, 2.0, 0.0)
    ) * factor
    for m, unit, radius, grad_unit in (
        (0, unit_img, radius_img, product(coupling, unit_txt, NN)),
        (1, unit_txt, radius_txt, product(coupling.T, unit_img, NN)),
    ):
        along = jnp.sum(unit * grad_unit, axis=1, keepdims=True)
        grad = (grad_unit - unit * along) / radius
        grads[m] = grad
        q = dot3(halves(grad), (m_large[m], m_small[m]), NT)
        back[m] = q.reshape(every.shape[0], n_z, q.shape[1])


def backward_kernel(n_z, n_dp, where, *refs):
    gated, slope, blocks = refs[:n_z], refs[n_z : 2 * n_z], refs[2 * n_z : 3 * n_z]
    meta, back, both, router_out = refs[3 * n_z :]
    lane = lax.broadcasted_iota(jnp.int32, (n_dp, LANES), 1)
    chosen = jnp.where(lane == where[1], 1.0, 0.0)
    slots = CAP * n_dp
    for r in range(n_z):
        plane = (where[0] + r) & (n_z - 1)
        back_img = back[0, :, pl.ds(plane, 1), :].reshape(n_dp, back.shape[3])
        back_txt = back[1, :, pl.ds(plane, 1), :].reshape(n_dp, back.shape[3])
        block = meta[plane]
        for slot in range(CAP):
            part = slice(slot * n_dp, (slot + 1) * n_dp)
            out = slice(r * slots + slot * n_dp, r * slots + (slot + 1) * n_dp)
            weight_img, weight_txt = slot_weights(block, float(slot))
            mixed = weight_img * back_img + weight_txt * back_txt
            both[out, LANES:] = slope[r][part, LANES:] * mixed
            log_gate = jnp.sum(gated[r][part, :] * mixed, axis=1, keepdims=True)
            both[out, :LANES] = log_gate * (chosen - slope[r][part, :LANES])
    total = 0.0
    for r in range(n_z):
        logits = both[r * slots : (r + 1) * slots, :LANES]
        total = total + dot3(halves(logits), halves(blocks[r][...]), TN)
    router_out[...] = total


def rows_kernel(which, where, both, w_large, w_small, *grad_rows):
    slots = grad_rows[0].shape[0]
    for r, out in zip(which, grad_rows):
        values = halves(both[r * slots : (r + 1) * slots, :])
        out[...] = dot3(values, (w_large[...], w_small[...]), NN)


def weight_kernel(where, both, *refs):
    blocks, out = refs[:-1], refs[-1]
    slots = blocks[0].shape[0]
    for r, rows in enumerate(blocks):
        values = halves(both[r * slots : (r + 1) * slots, LANES:])
        term = dot3(values, halves(rows[...]), TN)
        if r == 0:
            out[...] = term
        else:
            out[...] += term


def body(tokens, router_weight, expert_in, expert_out, projection, assignment, modality):
    tok_count, width = tokens.shape
    experts = router_weight.shape[1]
    n_dp = lax.axis_size("dp")
    n_z = lax.axis_size("expert")
    pairs = n_dp * n_z
    total_tokens = tok_count * pairs
    w_in = expert_in[0]
    w_out = expert_out[0]
    hidden_dev = w_in.shape[1]
    embed_width = projection.shape[2]
    my_dp = lax.axis_index("dp")
    my_z = lax.axis_index("expert")
    own_pair = my_dp * n_z + my_z
    where = jnp.stack([my_z, my_dp])
    my_core = my_dp & 1

    def step(values, shift):
        return lax.ppermute(values, "expert", [(i, (i + shift) % n_z) for i in range(n_z)])

    projection_mine = gather(jnp.where(my_core == 0, projection[0], projection[1]), "expert")
    projection_other = lax.ppermute(projection_mine, "dp", [(i, i ^ 1) for i in range(n_dp)])

    expert_ids = lax.broadcasted_iota(jnp.int32, (1, experts), 1)
    chosen_mask = (assignment[:, None] == expert_ids).astype(jnp.float32)
    before = (
        lax.broadcasted_iota(jnp.int32, (tok_count, tok_count), 0)
        > lax.broadcasted_iota(jnp.int32, (tok_count, tok_count), 1)
    ).astype(jnp.bfloat16)
    earlier = jnp.dot(
        before, chosen_mask.astype(jnp.bfloat16), preferred_element_type=jnp.float32
    )
    slot = jnp.sum(earlier * chosen_mask, axis=1).astype(jnp.int32)
    cell_ids = lax.broadcasted_iota(jnp.int32, (1, CAP * experts), 1)
    onehot = ((slot * experts + assignment)[:, None] == cell_ids).astype(jnp.float32)
    dispatched = mm_tn(onehot, tokens, highest).reshape(CAP, experts, width)
    received = a2a(dispatched, "dp", 1).reshape(CAP * n_dp, width)

    projection_img = jnp.where(my_core == 0, projection_mine, projection_other)
    projection_txt = jnp.where(my_core == 0, projection_other, projection_mine)
    mixed_img = mm(w_out, projection_img)
    mixed_txt = mm(w_out, projection_txt)
    mixed_first = after(mixed_img) + after(mixed_txt)
    half = received.shape[0] // 2
    left1, right1 = lax.optimization_barrier((step(received, -1), step(received, 1)))
    left2, right2 = lax.optimization_barrier((step(left1, -1), step(right1, 1)))
    left3, right3 = lax.optimization_barrier((step(left2, -1), step(right2, 1)))
    middle = jnp.concatenate(
        [step(left3[:half] + mixed_first, -1), step(right3[half:] + mixed_first, 1)], axis=0
    )
    blocks = [received, left1, left2, left3, middle, right3, right2, right1]

    logits = mm(tokens, router_weight, highest)
    exponent = jnp.exp(logits)
    router_prob = exponent / jnp.sum(exponent, axis=1, keepdims=True)
    is_image = (modality == 0).astype(jnp.float32)
    modal_mask = jnp.stack([is_image, 1.0 - is_image], axis=0)
    images = jnp.sum(is_image)
    group_sizes = jnp.stack([images, tok_count - images])
    usage_part = mm(modal_mask, router_prob, highest).reshape(1, 2 * experts)
    image_slots = dot(chosen_mask, is_image, ((0,), (0,)), highest)
    meta = jnp.concatenate(
        [
            image_slots[:, None],
            jnp.broadcast_to(images, (experts, 1)),
            jnp.broadcast_to(usage_part, (experts, 2 * experts)),
            received[:experts, : 126 - 2 * experts],
        ],
        axis=1,
    )
    meta = a2a(meta, "dp", 0)
    meta = a2a(jnp.broadcast_to(meta[None], (n_z, n_dp, 128)), "expert", 0)
    token_means = mm(modal_mask / group_sizes[:, None], tokens, highest)

    embed_means = jnp.concatenate(
        [mm(token_means[:1], projection_img), mm(token_means[1:], projection_txt)], axis=0
    )

    usage_all = jnp.sum(meta[:, :, 2 : 2 + 2 * experts], axis=(0, 1)).reshape(2, experts)
    image_total = jnp.sum(meta[:, :, 1])
    count_sum = jnp.stack([image_total, total_tokens - image_total])

    slots = CAP * n_dp
    w_pair = weight_halves(
        jnp.concatenate(
            [jnp.pad(router_weight.T, ((0, LANES - experts), (0, 0))), w_in.T], axis=0
        )
    )
    wide = LANES + hidden_dev
    done = [
        call(
            functools.partial(forward_kernel, experts),
            [(slots, hidden_dev), (slots, wide)],
            (where, blocks[r], *w_pair),
            us=2.5,
        )
        for r in range(n_z)
    ]

    mixed_pair = weight_halves(jnp.stack([mixed_img, mixed_txt]))
    part, sums = call(
        functools.partial(embed_kernel, n_z, n_dp),
        [(n_dp, 2 * n_z, embed_width), (2, n_dp, n_z, hidden_dev)],
        (where, *[d[0] for d in done], meta, *mixed_pair),
        us=3,
        mib=58,
        fetch=True,
    )
    sums = sums.reshape(2 * pairs, hidden_dev)
    column_ids = lax.broadcasted_iota(jnp.int32, (1, 2 * pairs), 1)
    pooled_part = (
        dot(w_out, sums, ((0,), (1,)))
        + jnp.where(column_ids == own_pair, token_means[0][:, None], 0.0)
        + jnp.where(column_ids == own_pair + pairs, token_means[1][:, None], 0.0)
    )
    pooled_cut = lax.psum_scatter(pooled_part, "expert", scatter_dimension=0, tiled=True)
    pooled_first = after(pooled_part)
    part = jnp.sum(a2a(part, "dp", 0), axis=0).reshape(2, n_z, embed_width)
    own_plane = lax.broadcasted_iota(jnp.int32, (1, n_z, 1), 1) == my_z
    part = part + jnp.where(own_plane, embed_means[:, None], 0.0) + pooled_first
    part = a2a(jnp.broadcast_to(part[None], (n_z, 2, n_z, embed_width)), "expert", 0)
    column = jnp.sum(part, axis=0).reshape(1, 2 * n_z, embed_width)
    every = a2a(jnp.broadcast_to(column, (n_dp, 2 * n_z, embed_width)), "dp", 0)
    pair_grads, back, contrast = call(
        functools.partial(
            head_kernel, n_z, contrast_scale * total_tokens / (2.0 * pairs)
        ),
        [(2, pairs, embed_width), (2, n_dp, n_z, hidden_dev), (8, LANES)],
        (where, every, *mixed_pair),
        us=5,
        mib=24,
    )
    grad_img, grad_txt = pair_grads[0], pair_grads[1]
    contrast = contrast[0, 0]

    both, router_sum = call(
        functools.partial(backward_kernel, n_z, n_dp),
        [(n_z * slots, wide), (LANES, width)],
        (where, *[d[0] for d in done], *[d[1] for d in done], *blocks, meta, back),
        us=8,
        mib=58,
        fetch=True,
    )
    grads = {}
    for which in ((4,), (3, 5), (2, 6), (1, 7, 0)):
        made = call(
            functools.partial(rows_kernel, which),
            [(slots, width)] * len(which),
            (where, both, *w_pair),
            us=1.8 * len(which),
        )
        grads.update(zip(which, made))

    mean_usage = usage_all / count_sum[:, None]
    log_usage = jnp.log(mean_usage)
    entropy_terms = jnp.sum(mean_usage * log_usage, axis=1)
    usage_factor = entropy_weight * total_tokens * (log_usage + 1.0) / count_sum[:, None]
    grad_prob = mm_tn(modal_mask, usage_factor, highest)
    grad_logits = router_prob * (
        grad_prob - jnp.sum(router_prob * grad_prob, axis=1, keepdims=True)
    )

    projection_part = jnp.concatenate(
        [mm(pooled_cut[:, :pairs], grad_img), mm(pooled_cut[:, pairs:], grad_txt)], axis=0
    )
    cut = projection_part.shape[0] // n_dp
    router_part = router_sum[:experts] + mm_tn(grad_logits, tokens)
    cut_router = -(-width // embed_width)
    router_part = jnp.pad(router_part, ((0, 0), (0, cut_router * embed_width - width)))
    shared = jnp.concatenate(
        [
            projection_part.reshape(n_dp, cut, embed_width),
            router_part.reshape(n_dp, cut_router, embed_width),
        ],
        axis=1,
    )
    shared = jnp.sum(a2a(shared, "dp", 0), axis=0)
    router_cut = a2a(
        jnp.broadcast_to(shared[None, cut:], (n_z, cut_router, embed_width)), "expert", 0
    )
    shared = jnp.concatenate([shared[:cut], jnp.sum(router_cut, axis=0)], axis=0)
    shared = a2a(jnp.broadcast_to(shared[None], (n_dp,) + shared.shape), "dp", 0)
    grad_projection = shared[:, :cut].reshape(projection.shape)
    grad_router = shared[:, cut:].reshape(n_dp, cut_router * embed_width)[:, :width].T

    (grad_in,) = call(
        weight_kernel,
        [(hidden_dev, width)],
        (where, both, *blocks),
        us=10,
        mib=58,
        fetch=True,
    )
    grad_expert_in = grad_in.T
    transfer_img = mm_tn(sums[:pairs], grad_img)
    transfer_txt = mm_tn(sums[pairs:], grad_txt)
    grad_expert_out = mm_nt(transfer_img, projection_img) + mm_nt(transfer_txt, projection_txt)

    farthest = grads[4]
    ahead, behind = lax.optimization_barrier((step(farthest[half:], 1), step(farthest[:half], -1)))
    ahead, behind = lax.optimization_barrier(
        (
            step(jnp.concatenate([grads[3][:half], grads[3][half:] + ahead], axis=0), 1),
            step(jnp.concatenate([grads[5][:half] + behind, grads[5][half:]], axis=0), -1),
        )
    )
    ahead, behind = lax.optimization_barrier(
        (step(grads[2] + ahead, 1), step(grads[6] + behind, -1))
    )
    ahead, behind = lax.optimization_barrier(
        (
            step(grads[1] + ahead, 1),
            step(grads[7] + behind, -1),
        )
    )
    grad_rows = grads[0] + ahead + behind
    grad_back = a2a(grad_rows.reshape(CAP, n_dp, width), "dp", 1).reshape(CAP * experts, width)
    grad_dispatch = mm(onehot, grad_back, highest)

    own_img = lax.dynamic_slice_in_dim(grad_img, own_pair, 1, 0)
    own_txt = lax.dynamic_slice_in_dim(grad_txt, own_pair, 1, 0)
    grad_pooled = jnp.concatenate(
        [mm_nt(own_img, projection_img), mm_nt(own_txt, projection_txt)], axis=0
    )
    grad_output = mm_tn(modal_mask, grad_pooled / group_sizes[:, None], highest)
    grad_tokens = grad_output + mm_nt(grad_logits, router_weight, highest) + grad_dispatch
    losses = jnp.stack([contrast, entropy_terms[0], entropy_terms[1]])
    return (
        losses,
        grad_tokens,
        grad_router,
        grad_expert_in[None],
        grad_expert_out[None],
        grad_projection,
    )


def solution(mesh):
    return jax.shard_map(
        body,
        mesh=mesh,
        in_specs=(
            P(("dp", "expert"), None),
            P(),
            P("dp", None, "expert"),
            P("dp", "expert", None),
            P(None, "expert", None),
            P(("dp", "expert")),
            P(("dp", "expert")),
        ),
        out_specs=(
            P(),
            P(("dp", "expert"), None),
            P(),
            P("dp", None, "expert"),
            P("dp", "expert", None),
            P(None, "expert", None),
        ),
        check_vma=False,
    )
```
